32 devices in a mesh: paths: 16 (over z, x, core), trades: 2 (over y).
Axes of the slice: x: 2, y: 2, z: 4, core: 2. Of those that a mesh axis runs over, the one named last changes fastest.
Arguments:
- basis: bfloat16 [16384, 512], P('paths'), may hold values from -6 to 6
- coef: bfloat16 [512, 4096], P('paths', 'trades'), may hold values from -0.25 to 0.25
- membership: int32 [4096, 512], P('trades'), may hold values from -1 to 1, as said below
- counts: int32 [512], replicated, may hold values from 1 to 15, as said below
- borrow: float32 [512], replicated, may hold values from 0.3 to 3
- lend: float32 [512], replicated, may hold values from 0.3 to 3
Outputs:
- d_basis: float32 [16384, 512], P(('paths', 'trades'))
- d_coef: float32 [512, 4096], P('paths', 'trades')
The draws below stay inside these ranges and needn't reach their ends.
Inputs may be any that keep to these rules, and one draw needn't show every extreme that they name: Each row of membership has exactly one nonzero entry, 1 or -1, and every set holds at least one trade. counts[s] is the number of nonzero entries in column s of membership; some set holds exactly one trade and some set exactly 15.
All inputs are finite; a program needn't handle non-finite values.
Results may differ from the reference program's by a relative error of at most 0.0042.
Values may be sent and summed in bfloat16 or wider, within the bound.
A program may use at most 64 MiB of HBM per device.

```python
import jax
import jax.numpy as jnp
from jax import lax

K = 512
SETS = 512
P_DEV = 1024
PATHS = 16384
NTRADES = 4096
N_PATHS = 16


def assign_sets(key):
    average = NTRADES // SETS
    half_sets = SETS // 2
    spread = jax.random.randint(jax.random.fold_in(key, 11), (half_sets,), 0, average)
    spread = jnp.where(jnp.arange(half_sets, dtype=jnp.int32) == 0, average - 1, spread).astype(jnp.int32)
    sizes = jnp.concatenate([average - spread, average + spread]).astype(jnp.int32)
    which = jax.random.permutation(jax.random.fold_in(key, 12), SETS)
    set_sizes = sizes[which].astype(jnp.int32)
    ends = jnp.cumsum(set_sizes).astype(jnp.int32)
    slots = jnp.arange(NTRADES, dtype=jnp.int32)
    owner = jnp.sum((ends[None, :] <= slots[:, None]).astype(jnp.int32), axis=1).astype(jnp.int32)
    order = jax.random.permutation(jax.random.fold_in(key, 13), NTRADES)
    owner = owner[order].astype(jnp.int32)
    signs = jax.random.randint(jax.random.fold_in(key, 14), (NTRADES,), 0, 2) * 2 - 1
    return (owner, signs.astype(jnp.int32))


def draw_membership(key, part):
    owner, signs = assign_sets(key)
    hit = jnp.arange(SETS, dtype=jnp.int32)[None, :] == owner[:, None]
    return jnp.where(hit, signs[:, None], 0).astype(jnp.int32)


def draw_counts(key, part):
    owner, signs = assign_sets(key)
    hit = jnp.arange(SETS, dtype=jnp.int32)[None, :] == owner[:, None]
    return jnp.sum(hit.astype(jnp.int32), axis=0).astype(jnp.int32)


def funding_spreads(key):
    upper_bit = jax.random.randint(jax.random.fold_in(key, 21), (SETS,), 0, 2)
    first = jax.random.uniform(jax.random.fold_in(key, 22), (SETS,), jnp.float32)
    second = jax.random.uniform(jax.random.fold_in(key, 23), (SETS,), jnp.float32)
    higher = jnp.exp(jnp.log(2.0) + (jnp.log(3.0) - jnp.log(2.0)) * first)
    lower = jnp.exp(jnp.log(0.3) + (jnp.log(0.6) - jnp.log(0.3)) * second)
    borrow_side = jnp.where(upper_bit == 1, higher, lower).astype(jnp.float32)
    lend_side = jnp.where(upper_bit == 1, lower, higher).astype(jnp.float32)
    return (borrow_side, lend_side)


def draw_borrow(key, part):
    borrow_side, lend_side = funding_spreads(key)
    return borrow_side.astype(jnp.float32)


def draw_lend(key, part):
    borrow_side, lend_side = funding_spreads(key)
    return lend_side.astype(jnp.float32)


def raised(entries, rng, source, target, parts, factor):
    owner, partner = [(jnp.arange(entries.shape[axis_at]) // (entries.shape[axis_at] // parts)).reshape([-1 if axis == axis_at else 1 for axis in range(entries.ndim)]) for axis_at in (source, target)]
    chosen = jax.random.permutation(rng, parts)[partner]
    strong = (owner == chosen) | (owner == (partner + parts // 2) % parts)
    return jnp.where(strong, factor * entries, entries)


def levels(own_key, extent, pieces, smallest, high):
    factor_of = 1.0
    for dim, parts in pieces:
        draws = jax.random.uniform(jax.random.fold_in(jax.random.fold_in(own_key, 6), dim), (parts,), jnp.float32, smallest / len(pieces), high / len(pieces))
        factor_of = factor_of * jnp.repeat(jnp.exp(draws), extent[dim] // parts).reshape((-1,) + (1,) * (len(extent) - 1 - dim))
    return factor_of


def noise(rng, shape, scale, bound, pieces=(), kind=jnp.bfloat16):
    array = scale * jax.random.normal(rng, shape, jnp.float32)
    if pieces:
        array = array * levels(rng, shape, pieces, -0.22, 0.18)
    return jnp.clip(array, -bound, bound).astype(kind)


def heavy_noise(own_key, shape, scale, most, cuts, heavy, kind=jnp.bfloat16):
    result = scale * jax.random.normal(own_key, shape, jnp.float32)
    if cuts:
        result = result * levels(own_key, shape, cuts, -0.22, 0.18)
    return jnp.clip(raised(result, jax.random.fold_in(own_key, 3), *heavy), -most, most).astype(kind)


def setup_inputs(seed: int = 0) -> dict:
    seeds = jax.random.split(jax.random.key(seed), 7)
    basis = heavy_noise(seeds[0], (PATHS, K), 1.0, 6.0, ((0, 16),), (0, 1, 16, 2.0))
    coef = noise(seeds[1], (K, NTRADES), K ** -0.5, 0.25, ((0, 16), (1, 2)))
    membership = draw_membership(jax.random.fold_in(seeds[6], 71), 0)
    counts = draw_counts(jax.random.fold_in(seeds[6], 71), 0)
    borrow = draw_borrow(jax.random.fold_in(seeds[6], 71), 0)
    lend = draw_lend(jax.random.fold_in(seeds[6], 71), 0)
    return dict(basis=basis, coef=coef, membership=membership, counts=counts, borrow=borrow, lend=lend)


def reference(basis, coef, membership, counts, borrow, lend):
    high = lax.Precision.HIGHEST
    member = membership.astype(jnp.float32)
    scale = 1.0 / jnp.sqrt(counts.astype(jnp.float32))
    coef_wide = coef.astype(jnp.float32)
    blocks = basis.reshape(N_PATHS, P_DEV, K)

    def step(carry, block):
        block_wide = block.astype(jnp.float32)
        trade_value = jnp.dot(block_wide, coef_wide, precision=high)
        exposure = jax.nn.softplus(trade_value).astype(jnp.bfloat16)
        netted = jnp.dot(exposure.astype(jnp.float32), member, precision=high)
        scaled = netted * scale
        set_grad = ((borrow * jax.nn.sigmoid(scaled) + lend * jax.nn.sigmoid(-scaled)) * scale).astype(jnp.bfloat16)
        trade_grad = jnp.dot(set_grad.astype(jnp.float32), member.T, precision=high)
        value_grad = (trade_grad * jax.nn.sigmoid(trade_value)).astype(jnp.bfloat16).astype(jnp.float32)
        d_block = jnp.dot(value_grad, coef_wide.T, precision=high)
        carry = carry + jnp.dot(block_wide.T, value_grad, precision=high)
        return (carry, d_block)
    total, d_blocks = lax.scan(step, jnp.zeros((K, NTRADES), jnp.float32), blocks)
    d_coef = total * (1.0 / jnp.sqrt(jnp.float32(PATHS)))
    return (d_blocks.reshape(PATHS, K), d_coef)
```

```python
import functools

import jax
import jax.numpy as jnp
from jax import lax
from jax.experimental import pallas as pl
from jax.experimental.pallas import tpu as pltpu
from jax.sharding import PartitionSpec as P

MESH = pl.DeviceIdType.MESH
VMEM = pl.BlockSpec(memory_space=pltpu.VMEM)


def place():
    p, y = lax.axis_index("paths"), lax.axis_index("trades")
    return p // 4, lax.rem(p // 2, 2), lax.rem(p, 2), y


def device(z, x, c, y):
    return (z * 4 + x * 2 + c, y)


def greet(z, x, c, y):
    barrier = pltpu.get_barrier_semaphore()
    others = [device(lax.rem(z + k, 4), x, c, y) for k in (1, 2, 3)]
    others += [device(z, 1 - x, c, y), device(z, x, 1 - c, y), device(z, x, c, 1 - y)]
    for other in others:
        pl.semaphore_signal(barrier, inc=1, device_id=other, device_id_type=MESH)
    pl.semaphore_wait(barrier, len(others))


def remote(src, dst, sems, i, target):
    return pltpu.make_async_remote_copy(
        src_ref=src,
        dst_ref=dst,
        send_sem=sems[0].at[i],
        recv_sem=sems[1].at[i],
        device_id=target,
        device_id_type=MESH,
    )


def gather_kernel(coef_ref, idx_ref, full_ref, idxo_ref, *sems):
    zs, xas, yas, xbs, ybs, cs, ids = [sems[2 * i : 2 * i + 2] for i in range(7)]
    z, x, c, y = place()
    rows, cols = coef_ref.shape
    half = cols // 2

    def block(zb, xb, yb, h=None):
        row = pl.multiple_of((zb * 4 + xb * 2 + c) * rows, rows)
        if h is None:
            return full_ref.at[pl.ds(row, rows), pl.ds(pl.multiple_of(yb * cols, cols), cols)]
        col = pl.multiple_of(yb * cols + h * half, half)
        return full_ref.at[pl.ds(row, rows), pl.ds(col, half)]

    greet(z, x, c, y)
    block(z, x, y)[...] = coef_ref[...]
    idxo_ref[y] = idx_ref[...]
    started = []

    def send(part, sems, i, target):
        copy = remote(part, part, sems, i, target)
        copy.start()
        started.append(copy)
        return copy

    to_x, to_y, to_c = device(z, 1 - x, c, y), device(z, x, c, 1 - y), device(z, x, 1 - c, y)
    zc = [send(block(z, x, y), zs, k - 1, device(lax.rem(z + k, 4), x, c, y)) for k in (1, 2, 3)]
    idx_copy = send(idxo_ref.at[y], ids, 0, to_y)
    line = [lax.rem(z + 4 - j, 4) for j in range(4)]
    xa, yb = [], []
    for j in range(4):
        if j:
            zc[j - 1].wait_recv()
        xa.append(send(block(line[j], x, y, 0), xas, j, to_x))
        yb.append(send(block(line[j], x, y, 1), ybs, j, to_y))
        send(block(line[j], x, y, 0), yas, j, to_y)
        send(block(line[j], x, y, 1), xbs, j, to_x)
        send(block(line[j], x, y), cs, j, to_c)
    for j in range(4):
        xa[j].wait_recv()
        send(block(line[j], 1 - x, y, 0), yas, 4 + j, to_y)
        send(block(line[j], 1 - x, y, 0), cs, 4 + j, to_c)
        yb[j].wait_recv()
        send(block(line[j], x, 1 - y, 1), xbs, 4 + j, to_x)
        send(block(line[j], x, 1 - y, 1), cs, 8 + j, to_c)
    for j in range(4):
        remote(block(line[j], x, y, 0), block(line[j], x, 1 - y, 0), yas, j, to_y).wait_recv()
        send(block(line[j], x, 1 - y, 0), cs, 12 + j, to_c)
        remote(block(line[j], x, y, 1), block(line[j], 1 - x, y, 1), xbs, j, to_x).wait_recv()
        send(block(line[j], 1 - x, y, 1), cs, 16 + j, to_c)
    for j in range(4):
        far = block(line[j], 1 - x, 1 - y, 0)
        remote(far, far, yas, 4 + j, to_y).wait_recv()
        send(far, cs, 20 + j, to_c)
        far = block(line[j], 1 - x, 1 - y, 1)
        remote(far, far, xbs, 4 + j, to_x).wait_recv()
        send(far, cs, 24 + j, to_c)
    idx_copy.wait_recv()
    for i in range(28):
        part = block(z, x, y) if i < 4 else block(z, x, y, 0)
        remote(part, part, cs, i, to_c).wait_recv()
    for copy in started:
        copy.wait_send()


def gather(coef, idx):
    rows, cols = coef.shape
    counts = (3, 4, 8, 8, 4, 28, 1)
    sems = [pltpu.SemaphoreType.DMA((n,)) for n in counts for _ in range(2)]
    return pl.pallas_call(
        gather_kernel,
        out_shape=(
            jax.ShapeDtypeStruct((rows * 16, cols * 2), coef.dtype),
            jax.ShapeDtypeStruct((2,) + idx.shape, idx.dtype),
        ),
        in_specs=[VMEM, VMEM],
        out_specs=(VMEM, VMEM),
        scratch_shapes=sems,
        compiler_params=pltpu.CompilerParams(
            collective_id=0, has_side_effects=True, vmem_limit_bytes=48 * 1024 * 1024
        ),
        name="coef_gather",
    )(coef, idx)


def reduce_kernel(factor, bt_ref, vg_ref, out_ref, cso, cri, acc, yso, yri, xso, xri, xbo, xbi, ybo, ybi, zso, zri, *sems):
    cs, yas, xas, xbs, ybs, zs = [sems[2 * i : 2 * i + 2] for i in range(6)]
    z, x, c, y = place()
    cols = out_ref.shape[1]
    width = cols // 4
    rows = out_ref.shape[0]
    side = rows * 4
    greet(z, x, c, y)
    to_x, to_y, to_c = device(z, 1 - x, c, y), device(z, x, c, 1 - y), device(z, x, 1 - c, y)
    mine, theirs = pl.ds(pl.multiple_of(x * side, side), side), pl.ds(pl.multiple_of((1 - x) * side, side), side)
    started = []

    def send(src, dst, sems, i, target):
        copy = remote(src, dst, sems, i, target)
        copy.start()
        started.append(copy)
        return copy

    def number(h, s, q):
        return (h * 2 + s) * 2 + q

    def term(core, h, s, q):
        yq = y if q else 1 - y
        col = pl.multiple_of(yq * cols + (h * 2 + s) * width, width)
        return jnp.dot(bt_ref[core], vg_ref[:, pl.ds(col, width)], preferred_element_type=jnp.float32)

    order = [(h, s, q) for s in (0, 1) for h, q in ((0, 0), (1, 0), (1, 1), (0, 1))]
    copies = {}
    for h, s, q in order:
        i = number(h, s, q)
        cso[i] = term(1 - c, h, s, q).astype(jnp.bfloat16)
        copies["c", i] = send(cso.at[i], cri.at[i], cs, i, to_c)
    for h, s, q in order:
        i = number(h, s, q)
        own = term(c, h, s, q)
        copies["c", i].wait_recv()
        acc[i] = own + cri[i].astype(jnp.float32)
        if h == 0 and q == 0:
            yso[s] = acc[i].astype(jnp.bfloat16)
            copies["ya", s] = send(yso.at[s], yri.at[s], yas, s, to_y)
        if h == 1:
            j = q * 2 + s
            xbo[j] = acc[i, theirs].astype(jnp.bfloat16)
            copies["xb", j] = send(xbo.at[j], xbi.at[j], xbs, j, to_x)
    for s in (0, 1):
        i = number(1, s, 0)
        copies["xb", s].wait_recv()
        ybo[s] = (acc[i, mine] + xbi[s].astype(jnp.float32)).astype(jnp.bfloat16)
        copies["yb", s] = send(ybo.at[s], ybi.at[s], ybs, s, to_y)
        i = number(0, s, 1)
        copies["ya", s].wait_recv()
        xso[s] = (acc[i, theirs] + yri[s, theirs].astype(jnp.float32)).astype(jnp.bfloat16)
        copies["xa", s] = send(xso.at[s], xri.at[s], xas, s, to_x)
        acc[i, mine] = acc[i, mine] + yri[s, mine].astype(jnp.float32)
        i = number(1, s, 1)
        copies["xb", 2 + s].wait_recv()
        acc[i, mine] = acc[i, mine] + xbi[2 + s].astype(jnp.float32)
    for s in (0, 1):
        for h in (1, 0):
            i, j = number(h, s, 1), h * 2 + s
            copies["yb" if h else "xa", s].wait_recv()
            arrived = ybi[s] if h else xri[s]
            acc[i, mine] = acc[i, mine] + arrived.astype(jnp.float32)
            zso[j] = acc[i, mine].astype(jnp.bfloat16)
            for k in (1, 2, 3):
                zk = lax.rem(z + k, 4)
                part = zso.at[j, pl.ds(pl.multiple_of(zk * rows, rows), rows)]
                n = (k - 1) * 4 + j
                copies["z", n] = send(part, zri.at[n], zs, n, device(zk, x, c, y))
    for s in (0, 1):
        for h in (1, 0):
            i, j = number(h, s, 1), h * 2 + s
            total = acc[i, pl.ds(pl.multiple_of(x * side + z * rows, rows), rows)]
            for k in range(3):
                copies["z", k * 4 + j].wait_recv()
                total = total + zri[k * 4 + j].astype(jnp.float32)
            out_ref[:, pl.ds(j * width, width)] = total * factor
    for copy in started:
        copy.wait_send()


def reduce_coef(bt, vg, factor, rows, cols):
    side, width = rows * 4, cols // 4
    b, f = jnp.bfloat16, jnp.float32
    buffers = [
        ((8, 2 * side, width), b), ((8, 2 * side, width), b), ((8, 2 * side, width), f),
        ((2, 2 * side, width), b), ((2, 2 * side, width), b),
        ((2, side, width), b), ((2, side, width), b),
        ((4, side, width), b), ((4, side, width), b),
        ((2, side, width), b), ((2, side, width), b),
        ((4, side, width), b), ((12, rows, width), b),
    ]
    sems = [pltpu.SemaphoreType.DMA((n,)) for n in (8, 2, 2, 4, 2, 12) for _ in range(2)]
    return pl.pallas_call(
        functools.partial(reduce_kernel, factor),
        out_shape=jax.ShapeDtypeStruct((rows, cols), f),
        in_specs=[VMEM, VMEM],
        out_specs=VMEM,
        scratch_shapes=[pltpu.VMEM(shape, kind) for shape, kind in buffers] + sems,
        compiler_params=pltpu.CompilerParams(
            collective_id=1, has_side_effects=True, vmem_limit_bytes=48 * 1024 * 1024
        ),
        name="coef_reduce",
    )(bt, vg)


def funding(netted, scale, borrow, lend):
    scaled = netted * scale
    grad = (borrow * jax.nn.sigmoid(scaled) + lend * jax.nn.sigmoid(-scaled)) * scale
    return grad.astype(jnp.bfloat16)


def body(basis, coef, membership, counts, borrow, lend):
    trades, sets = membership.shape
    rows, cols = coef.shape
    paths = basis.shape[0] // 2
    number = jnp.arange(1, sets + 1, dtype=jnp.int32)
    signed = jnp.sum(membership * number, axis=1, dtype=jnp.int32)
    coef_full, signed_all = gather(coef, signed.reshape(trades // 128, 128))
    signed_all = signed_all.reshape(2 * trades, 1)
    member = jnp.where(jnp.abs(signed_all) == number, jnp.sign(signed_all), 0).astype(jnp.bfloat16)
    half = lax.dynamic_slice_in_dim(basis, lax.axis_index("trades") * paths, paths, 0)
    trade_value = jnp.dot(half, coef_full, preferred_element_type=jnp.float32)
    exposure = jax.nn.softplus(trade_value).astype(jnp.bfloat16)
    netted = jnp.dot(exposure, member, preferred_element_type=jnp.float32)
    set_grad = funding(netted, lax.rsqrt(counts.astype(jnp.float32)), borrow, lend)
    trade_grad = lax.dot_general(
        set_grad, member, (((1,), (1,)), ((), ())), preferred_element_type=jnp.float32
    )
    value_grad = (trade_grad * jax.nn.sigmoid(trade_value)).astype(jnp.bfloat16)
    d_basis = lax.dot_general(
        value_grad, coef_full, (((1,), (1,)), ((), ())), preferred_element_type=jnp.float32
    )
    bt = half.T.reshape(4, 2, 2, rows, paths).transpose(2, 1, 0, 3, 4).reshape(2, 8 * rows, paths)
    factor = (basis.shape[0] * lax.axis_size("paths")) ** -0.5
    d_coef = reduce_coef(bt, value_grad, factor, rows, cols)
    return (d_basis, d_coef)


def body_any(basis, coef, membership, counts, borrow, lend):
    path_rows = basis.shape[0]
    member = membership.astype(jnp.bfloat16)
    coef_full = lax.all_gather(coef, "paths", axis=0, tiled=True)
    trade_value = jnp.dot(basis, coef_full, preferred_element_type=jnp.float32)
    exposure = jax.nn.softplus(trade_value).astype(jnp.bfloat16)
    partial_net = jnp.dot(exposure, member, preferred_element_type=jnp.float32)
    scale_all = lax.rsqrt(counts.astype(jnp.float32))
    net_share = lax.psum_scatter(partial_net, "trades", scatter_dimension=1, tiled=True)
    width_sets = net_share.shape[1]
    offset_sets = lax.axis_index("trades") * width_sets
    grad_share = funding(
        net_share,
        lax.dynamic_slice_in_dim(scale_all, offset_sets, width_sets, 0),
        lax.dynamic_slice_in_dim(borrow, offset_sets, width_sets, 0),
        lax.dynamic_slice_in_dim(lend, offset_sets, width_sets, 0),
    )
    set_grad = lax.all_gather(grad_share, "trades", axis=1, tiled=True)
    trade_grad = lax.dot_general(
        set_grad, member, (((1,), (1,)), ((), ())), preferred_element_type=jnp.float32
    )
    value_grad = (trade_grad * jax.nn.sigmoid(trade_value)).astype(jnp.bfloat16)
    d_basis = lax.psum_scatter(
        lax.dot_general(
            value_grad, coef_full, (((1,), (1,)), ((), ())), preferred_element_type=jnp.float32
        ),
        "trades",
        scatter_dimension=0,
        tiled=True,
    )
    factor = 1.0 / jnp.sqrt(jnp.float32(path_rows * lax.axis_size("paths")))
    product = lax.dot_general(
        basis, value_grad, (((0,), (0,)), ((), ())), preferred_element_type=jnp.float32
    )
    d_coef = lax.psum_scatter(product * factor, "paths", scatter_dimension=0, tiled=True)
    return (d_basis, d_coef)


def solution(mesh):
    placed = (P("paths", None), P("paths", "trades"), P("trades", None), P(), P(), P())
    small = (mesh.shape["paths"], mesh.shape["trades"]) == (16, 2)
    return jax.shard_map(
        body if small else body_any,
        mesh=mesh,
        in_specs=placed,
        out_specs=(P(("paths", "trades"), None), P("paths", "trades")),
        check_vma=False,
    )
```

```python
import functools

import jax
import jax.numpy as jnp
from jax import lax
from jax.experimental import pallas as pl
from jax.experimental.pallas import tpu as pltpu
from jax.sharding import PartitionSpec as P

MESH = pl.DeviceIdType.MESH
VMEM = pl.BlockSpec(memory_space=pltpu.VMEM)


def place():
    p, y = lax.axis_index("paths"), lax.axis_index("trades")
    return p // 4, lax.rem(p // 2, 2), lax.rem(p, 2), y


def device(z, x, c, y):
    return (z * 4 + x * 2 + c, y)


def greet(z, x, c, y):
    barrier = pltpu.get_barrier_semaphore()
    others = [device(lax.rem(z + k, 4), x, c, y) for k in (1, 2, 3)]
    others += [device(z, 1 - x, c, y), device(z, x, 1 - c, y), device(z, x, c, 1 - y)]
    for other in others:
        pl.semaphore_signal(barrier, inc=1, device_id=other, device_id_type=MESH)
    pl.semaphore_wait(barrier, len(others))


def remote(src, dst, sems, i, target):
    return pltpu.make_async_remote_copy(
        src_ref=src,
        dst_ref=dst,
        send_sem=sems[0].at[i],
        recv_sem=sems[1].at[i],
        device_id=target,
        device_id_type=MESH,
    )


NT = (((1,), (1,)), ((), ()))


def adjoint_kernel(
    factor, member_ref, coef_ref, half_ref, bt_ref, spread_ref, db_ref, out_ref,
    member, full_ref, idxo, mem_t, sig, exposure, netted, set_grad, vg,
    cso, cri, acc, yso, yri, xso, xri, xbo, xbi, ybo, ybi, zso, zri, member_sem, *sems
):
    gz, gxa, gya, gxb, gyb, gc, gi, cs, yas, xas, xbs, ybs, zs = [sems[2 * i : 2 * i + 2] for i in range(13)]
    z, x, c, y = place()
    rows, cols = coef_ref.shape
    half = cols // 2
    paths, sets = netted.shape
    f32, bf16 = jnp.float32, jnp.bfloat16
    started = []

    fetch = pltpu.make_async_copy(member_ref, member, member_sem)
    fetch.start()

    def block(zb, xb, yb, h=None):
        row = pl.multiple_of((zb * 4 + xb * 2 + c) * rows, rows)
        if h is None:
            return full_ref.at[pl.ds(row, rows), pl.ds(pl.multiple_of(yb * cols, cols), cols)]
        col = pl.multiple_of(yb * cols + h * half, half)
        return full_ref.at[pl.ds(row, rows), pl.ds(col, half)]

    def send(src, dst, sems, i, target):
        copy = remote(src, dst, sems, i, target)
        copy.start()
        started.append(copy)
        return copy

    def pass_on(part, sems, i, target):
        return send(part, part, sems, i, target)

    to_x, to_y, to_c = device(z, 1 - x, c, y), device(z, x, c, 1 - y), device(z, x, 1 - c, y)
    block(z, x, y)[...] = coef_ref[...]
    greet(z, x, c, y)

    near = z + 1 - 2 * lax.rem(z, 2)
    line = [z, near, lax.rem(z + 2, 4), lax.rem(near + 2, 4)]
    zc = [pass_on(block(z, x, y), gz, k, device(line[k + 1], x, c, y)) for k in range(3)]

    def spread_own(j):
        a = pass_on(block(line[j], x, y, 0), gxa, j, to_x)
        b = pass_on(block(line[j], x, y, 1), gyb, j, to_y)
        pass_on(block(line[j], x, y, 0), gya, j, to_y)
        pass_on(block(line[j], x, y, 1), gxb, j, to_x)
        pass_on(block(line[j], x, y), gc, j, to_c)
        return a, b

    own = [spread_own(0)]

    fetch.wait()
    number = lax.broadcasted_iota(jnp.int32, (16, sets), 1) + 1
    first = lax.broadcasted_iota(jnp.int32, (16, sets), 0) == 0
    digits = jnp.where(first, number // 64, lax.rem(number, 64)).astype(f32).astype(bf16)

    def find(k, carry):
        at = pl.ds(pl.multiple_of(k * 512, 512), 512)
        both = lax.dot_general(
            digits, member[at, :].astype(f32).astype(bf16), NT, preferred_element_type=f32
        )
        idxo[y, :, at] = jnp.broadcast_to(both[0:1] * 64.0 + both[1:2], (8, 512))
        return carry

    lax.fori_loop(0, cols // 512, find, 0)
    idx_copy = pass_on(idxo.at[y], gi, 0, to_y)

    def build(yb):
        def chunk(k, carry):
            at = pl.ds(pl.multiple_of(k * 512, 512), 512)
            to = pl.ds(pl.multiple_of(yb * cols + k * 512, 512), 512)
            idx = idxo[yb, 0:1, at]
            size, sign = jnp.abs(idx), jnp.where(idx > 0, 1.0, -1.0)

            def some(r, inner):
                base = lax.broadcasted_iota(jnp.int32, (32, 512), 0) + (r * 32 + 1)
                hit = jnp.where(base.astype(f32) == size, sign, 0.0)
                mem_t[pl.ds(pl.multiple_of(r * 32, 32), 32), to] = hit.astype(bf16)
                return inner

            return lax.fori_loop(0, sets // 32, some, carry)

        lax.fori_loop(0, cols // 512, chunk, 0)

    def forward(yb, start, stop):
        def chunk(k, carry):
            at = pl.ds(pl.multiple_of(yb * cols + k * 512, 512), 512)
            sig[:, at] = jnp.dot(half_ref[...], full_ref[:, at], preferred_element_type=f32)

            def some(r, inner):
                part = pl.ds(pl.multiple_of(r * 32, 32), 32)
                v = sig[part, at]
                e = jnp.exp(-jnp.abs(v))
                log = jnp.where(e < 0.01, e * (1.0 - e * (0.5 - e * (1.0 / 3.0))), jnp.log(1.0 + e))
                exposure[part, :] = (jnp.maximum(v, 0.0) + log).astype(bf16)
                sig[part, at] = jnp.where(v >= 0, 1.0, e) / (1.0 + e)
                return inner

            lax.fori_loop(0, paths // 32, some, 0)
            netted[...] += lax.dot_general(exposure[...], mem_t[:, at], NT, preferred_element_type=f32)
            return carry

        lax.fori_loop(start, stop, chunk, 0)

    netted[...] = jnp.zeros_like(netted)
    for j in (1, 2, 3):
        zc[j - 1].wait_recv()
        own.append(spread_own(j))
    for j in range(4):
        own[j][0].wait_recv()
        pass_on(block(line[j], 1 - x, y, 0), gya, 4 + j, to_y)
        pass_on(block(line[j], 1 - x, y, 0), gc, 4 + j, to_c)
        own[j][1].wait_recv()
        pass_on(block(line[j], x, 1 - y, 1), gxb, 4 + j, to_x)
        pass_on(block(line[j], x, 1 - y, 1), gc, 8 + j, to_c)

    def landed(part, sems, i):
        remote(part, part, sems, i, to_c).wait_recv()
        return part

    def from_core(numbers):
        for i in numbers:
            landed(block(z, x, y) if i < 4 else block(z, x, y, 0), gc, i)

    for j in range(4):
        pass_on(landed(block(line[j], 1 - x, y, 1), gxb, j), gc, 16 + j, to_c)
    build(y)
    for j in range(4):
        pass_on(landed(block(line[j], x, 1 - y, 0), gya, j), gc, 12 + j, to_c)
    from_core([0, 1, 2, 3, 4, 5, 6, 7, 16, 17, 18, 19])
    forward(y, 0, 2)

    def far(j):
        pass_on(landed(block(line[j], 1 - x, 1 - y, 0), gya, 4 + j), gc, 20 + j, to_c)
        pass_on(landed(block(line[j], 1 - x, 1 - y, 1), gxb, 4 + j), gc, 24 + j, to_c)

    far(0)
    far(1)
    idx_copy.wait_recv()
    build(1 - y)
    far(2)
    far(3)
    forward(y, 2, 4)
    from_core([8, 9, 10, 11, 12, 13, 14, 15, 20, 21, 22, 23, 24, 25, 26, 27])
    forward(1 - y, 0, 4)

    def fund(r, carry):
        part = pl.ds(pl.multiple_of(r * 32, 32), 32)
        scale, borrow, lend = spread_ref[0:1, :], spread_ref[1:2, :], spread_ref[2:3, :]
        s = netted[part, :] * scale
        e = jnp.exp(-jnp.abs(s))
        grad = jnp.where(s >= 0, borrow + lend * e, borrow * e + lend) / (1.0 + e) * scale
        set_grad[part, :] = grad.astype(bf16)
        return carry

    lax.fori_loop(0, paths // 32, fund, 0)

    steps = 4
    width = half // steps
    side = rows * 4
    mine, theirs = pl.ds(pl.multiple_of(x * side, side), side), pl.ds(pl.multiple_of((1 - x) * side, side), side)
    copies = {}

    def columns(s, i):
        q = i // 2
        h = lax.rem((i + 1) // 2, 2)
        yq = (1 - y) + q * (2 * y - 1)
        return pl.ds(pl.multiple_of(yq * cols + h * half + s * width, width), width)

    def core_copy(n):
        return remote(cso.at[n], cri.at[n], cs, n, to_c)

    def first_step(s):
        def chunk(i, carry):
            at = columns(s, i)
            grad = jnp.dot(set_grad[...], mem_t[:, at], preferred_element_type=f32)
            vg[:, at] = (grad * sig[:, at]).astype(bf16)
            n = s * 4 + i
            cso[n] = jnp.dot(bt_ref[1 - c], vg[:, at], preferred_element_type=f32).astype(bf16)
            core_copy(n).start()
            return carry

        lax.fori_loop(0, 4, chunk, 0)

    def second_step(s):
        def chunk(i, carry):
            n = s * 4 + i
            own = jnp.dot(bt_ref[c], vg[:, columns(s, i)], preferred_element_type=f32)
            core_copy(n).wait_recv()
            acc[n] = own + cri[n].astype(f32)
            return carry

        lax.fori_loop(0, 4, chunk, 0)
        yso[s] = acc[s * 4].astype(bf16)
        copies["ya", s] = send(yso.at[s], yri.at[s], yas, s, to_y)
        for q in (0, 1):
            j = q * steps + s
            xbo[j] = acc[s * 4 + 1 + q, theirs].astype(bf16)
            copies["xb", j] = send(xbo.at[j], xbi.at[j], xbs, j, to_x)

    def third_step(s):
        copies["xb", s].wait_recv()
        ybo[s] = (acc[s * 4 + 1, mine] + xbi[s].astype(f32)).astype(bf16)
        copies["yb", s] = send(ybo.at[s], ybi.at[s], ybs, s, to_y)
        copies["ya", s].wait_recv()
        xso[s] = (acc[s * 4 + 3, theirs] + yri[s, theirs].astype(f32)).astype(bf16)
        copies["xa", s] = send(xso.at[s], xri.at[s], xas, s, to_x)
        acc[s * 4 + 3, mine] = acc[s * 4 + 3, mine] + yri[s, mine].astype(f32)
        copies["xb", steps + s].wait_recv()
        acc[s * 4 + 2, mine] = acc[s * 4 + 2, mine] + xbi[steps + s].astype(f32)

    def fourth_step(s):
        for h in (1, 0):
            i, j = s * 4 + (2 if h else 3), h * steps + s
            copies["yb" if h else "xa", s].wait_recv()
            arrived = ybi[s] if h else xri[s]
            acc[i, mine] = acc[i, mine] + arrived.astype(f32)
            zso[j] = acc[i, mine].astype(bf16)
            for k in range(3):
                zk = line[k + 1]
                part = zso.at[j, pl.ds(pl.multiple_of(zk * rows, rows), rows)]
                n = k * 2 * steps + j
                copies["z", n] = send(part, zri.at[n], zs, n, device(zk, x, c, y))

    def last_step(s):
        for h in (1, 0):
            i, j = s * 4 + (2 if h else 3), h * steps + s
            total = acc[i, pl.ds(pl.multiple_of(x * side + z * rows, rows), rows)]
            for k in range(3):
                copies["z", k * 2 * steps + j].wait_recv()
                total = total + zri[k * 2 * steps + j].astype(f32)
            out_ref[:, pl.ds(j * width, width)] = total * factor

    def basis_part(k):
        size = sets_k // 2
        db_ref[:, k * size : (k + 1) * size] = lax.dot_general(
            vg[...], full_ref[k * size : (k + 1) * size, :], NT, preferred_element_type=f32
        )

    sets_k = full_ref.shape[0]
    first_step(0)
    first_step(1)
    second_step(0)
    first_step(2)
    second_step(1)
    third_step(0)
    first_step(3)
    second_step(2)
    fourth_step(0)
    third_step(1)
    second_step(3)
    third_step(2)
    fourth_step(1)
    basis_part(0)
    third_step(3)
    fourth_step(2)
    basis_part(1)
    fourth_step(3)
    for s in range(steps):
        last_step(s)

    def sent(n, carry):
        core_copy(n).wait_send()
        return carry

    lax.fori_loop(0, 4 * steps, sent, 0)
    for copy in started:
        copy.wait_send()


def adjoint(membership, coef, half, bt, spread, factor):
    trades, sets = membership.shape
    rows, cols = coef.shape
    paths, k = half.shape
    b, f = jnp.bfloat16, jnp.float32
    steps = 4
    width, side = cols // 2 // steps, rows * 4
    buffers = [
        ((trades, sets), membership.dtype), ((k, 2 * cols), b), ((2, 8, cols), f), ((sets, 2 * cols), b),
        ((paths, 2 * cols), f), ((paths, 512), b), ((paths, sets), f), ((paths, sets), b), ((paths, 2 * cols), b),
        ((4 * steps, 2 * side, width), b), ((4 * steps, 2 * side, width), b), ((4 * steps, 2 * side, width), f),
        ((steps, 2 * side, width), b), ((steps, 2 * side, width), b),
        ((steps, side, width), b), ((steps, side, width), b),
        ((2 * steps, side, width), b), ((2 * steps, side, width), b),
        ((steps, side, width), b), ((steps, side, width), b),
        ((2 * steps, side, width), b), ((6 * steps, rows, width), b),
    ]
    counts = (3, 4, 8, 8, 4, 28, 1, 4 * steps, steps, steps, 2 * steps, steps, 6 * steps)
    sems = [pltpu.SemaphoreType.DMA((n,)) for n in counts for _ in range(2)]
    return pl.pallas_call(
        functools.partial(adjoint_kernel, factor),
        out_shape=(jax.ShapeDtypeStruct((paths, k), f), jax.ShapeDtypeStruct((rows, cols), f)),
        in_specs=[pl.BlockSpec(memory_space=pl.ANY)] + [VMEM] * 4,
        out_specs=(VMEM, VMEM),
        scratch_shapes=[pltpu.VMEM(shape, kind) for shape, kind in buffers] + [pltpu.SemaphoreType.DMA] + sems,
        compiler_params=pltpu.CompilerParams(
            collective_id=0, has_side_effects=True, vmem_limit_bytes=56 * 1024 * 1024
        ),
        name="adjoint",
    )(membership, coef, half, bt, spread)


def funding(netted, scale, borrow, lend):
    scaled = netted * scale
    grad = (borrow * jax.nn.sigmoid(scaled) + lend * jax.nn.sigmoid(-scaled)) * scale
    return grad.astype(jnp.bfloat16)


def body(basis, coef, membership, counts, borrow, lend):
    rows = coef.shape[0]
    paths = basis.shape[0] // 2
    half = lax.dynamic_slice_in_dim(basis, lax.axis_index("trades") * paths, paths, 0)
    bt = half.T.reshape(4, 2, 2, rows, paths).transpose(2, 1, 0, 3, 4).reshape(2, 8 * rows, paths)
    spread = jnp.stack([lax.rsqrt(counts.astype(jnp.float32)), borrow, lend])
    factor = (basis.shape[0] * lax.axis_size("paths")) ** -0.5
    return adjoint(membership, coef, half, bt, spread, factor)


def body_any(basis, coef, membership, counts, borrow, lend):
    path_rows = basis.shape[0]
    member = membership.astype(jnp.bfloat16)
    coef_full = lax.all_gather(coef, "paths", axis=0, tiled=True)
    trade_value = jnp.dot(basis, coef_full, preferred_element_type=jnp.float32)
    exposure = jax.nn.softplus(trade_value).astype(jnp.bfloat16)
    partial_net = jnp.dot(exposure, member, preferred_element_type=jnp.float32)
    scale_all = lax.rsqrt(counts.astype(jnp.float32))
    net_share = lax.psum_scatter(partial_net, "trades", scatter_dimension=1, tiled=True)
    width_sets = net_share.shape[1]
    offset_sets = lax.axis_index("trades") * width_sets
    grad_share = funding(
        net_share,
        lax.dynamic_slice_in_dim(scale_all, offset_sets, width_sets, 0),
        lax.dynamic_slice_in_dim(borrow, offset_sets, width_sets, 0),
        lax.dynamic_slice_in_dim(lend, offset_sets, width_sets, 0),
    )
    set_grad = lax.all_gather(grad_share, "trades", axis=1, tiled=True)
    trade_grad = lax.dot_general(
        set_grad, member, (((1,), (1,)), ((), ())), preferred_element_type=jnp.float32
    )
    value_grad = (trade_grad * jax.nn.sigmoid(trade_value)).astype(jnp.bfloat16)
    d_basis = lax.psum_scatter(
        lax.dot_general(
            value_grad, coef_full, (((1,), (1,)), ((), ())), preferred_element_type=jnp.float32
        ),
        "trades",
        scatter_dimension=0,
        tiled=True,
    )
    factor = 1.0 / jnp.sqrt(jnp.float32(path_rows * lax.axis_size("paths")))
    product = lax.dot_general(
        basis, value_grad, (((0,), (0,)), ((), ())), preferred_element_type=jnp.float32
    )
    d_coef = lax.psum_scatter(product * factor, "paths", scatter_dimension=0, tiled=True)
    return (d_basis, d_coef)


def solution(mesh):
    placed = (P("paths", None), P("paths", "trades"), P("trades", None), P(), P(), P())
    small = (mesh.shape["paths"], mesh.shape["trades"]) == (16, 2)
    return jax.shard_map(
        body if small else body_any,
        mesh=mesh,
        in_specs=placed,
        out_specs=(P(("paths", "trades"), None), P("paths", "trades")),
        check_vma=False,
    )
```

```python
import jax
import jax.numpy as jnp
from jax import lax
from jax.experimental import pallas as pl
from jax.experimental.pallas import tpu as pltpu
from jax.sharding import PartitionSpec as P

MESH = pl.DeviceIdType.MESH
VMEM = pl.BlockSpec(memory_space=pltpu.VMEM)


def place():
    p, y = lax.axis_index("paths"), lax.axis_index("trades")
    return p // 4, lax.rem(p // 2, 2), lax.rem(p, 2), y


def device(z, x, c, y):
    return (z * 4 + x * 2 + c, y)


def greet(z, x, c, y):
    barrier = pltpu.get_barrier_semaphore()
    others = [device(lax.rem(z + k, 4), x, c, y) for k in (1, 2, 3)]
    others += [device(z, 1 - x, c, y), device(z, x, 1 - c, y), device(z, x, c, 1 - y)]
    for other in others:
        pl.semaphore_signal(barrier, inc=1, device_id=other, device_id_type=MESH)
    pl.semaphore_wait(barrier, len(others))


def remote(src, dst, sems, i, target):
    return pltpu.make_async_remote_copy(
        src_ref=src,
        dst_ref=dst,
        send_sem=sems[0].at[i],
        recv_sem=sems[1].at[i],
        device_id=target,
        device_id_type=MESH,
    )


NT = (((1,), (1,)), ((), ()))


def adjoint_kernel(
    member_ref, basis_ref, coef_ref, counts_ref, borrow_ref, lend_ref, db_ref, out_ref,
    member, half_ref, bt_ref, full_ref, idxo, mem_t, sig, exposure, netted, set_grad, vg,
    cso, cri, acc, yso, yri, xso, xri, xbo, xbi, ybo, ybi, zso, zri, member_sem, half_sem, *sems
):
    gz, gxa, gya, gxb, gyb, gc, gi, cs, yas, xas, xbs, ybs, zs = [sems[2 * i : 2 * i + 2] for i in range(13)]
    z, x, c, y = place()
    rows, cols = coef_ref.shape
    half = cols // 2
    paths, sets = netted.shape
    f32, bf16 = jnp.float32, jnp.bfloat16
    started = []

    fetch = pltpu.make_async_copy(member_ref, member, member_sem)
    fetch.start()
    fetch_half = pltpu.make_async_copy(
        basis_ref.at[pl.ds(pl.multiple_of(y * paths, paths), paths)], half_ref, half_sem
    )
    fetch_half.start()

    def block(zb, xb, yb, h=None):
        row = pl.multiple_of((zb * 4 + xb * 2 + c) * rows, rows)
        if h is None:
            return full_ref.at[pl.ds(row, rows), pl.ds(pl.multiple_of(yb * cols, cols), cols)]
        col = pl.multiple_of(yb * cols + h * half, half)
        return full_ref.at[pl.ds(row, rows), pl.ds(col, half)]

    def send(src, dst, sems, i, target):
        copy = remote(src, dst, sems, i, target)
        copy.start()
        started.append(copy)
        return copy

    def pass_on(part, sems, i, target):
        return send(part, part, sems, i, target)

    to_x, to_y, to_c = device(z, 1 - x, c, y), device(z, x, c, 1 - y), device(z, x, 1 - c, y)
    block(z, x, y)[...] = coef_ref[...]
    greet(z, x, c, y)

    near = z + 1 - 2 * lax.rem(z, 2)
    line = [z, near, lax.rem(z + 2, 4), lax.rem(near + 2, 4)]
    zc = [pass_on(block(z, x, y), gz, k, device(line[k + 1], x, c, y)) for k in range(3)]

    def spread_own(j):
        a = pass_on(block(line[j], x, y, 0), gxa, j, to_x)
        b = pass_on(block(line[j], x, y, 1), gyb, j, to_y)
        pass_on(block(line[j], x, y, 0), gya, j, to_y)
        pass_on(block(line[j], x, y, 1), gxb, j, to_x)
        pass_on(block(line[j], x, y), gc, j, to_c)
        return a, b

    own = [spread_own(0)]

    number = lax.broadcasted_iota(jnp.int32, (16, sets), 1) + 1
    first = lax.broadcasted_iota(jnp.int32, (16, sets), 0) == 0
    digits = jnp.where(first, number // 64, lax.rem(number, 64)).astype(f32).astype(bf16)

    def find(k, carry):
        at = pl.ds(pl.multiple_of(k * 512, 512), 512)
        both = lax.dot_general(
            digits, member[at, :].astype(f32).astype(bf16), NT, preferred_element_type=f32
        )
        idxo[y, :, at] = jnp.broadcast_to(both[0:1] * 64.0 + both[1:2], (8, 512))
        return carry


    def build(yb):
        def chunk(k, carry):
            at = pl.ds(pl.multiple_of(k * 512, 512), 512)
            to = pl.ds(pl.multiple_of(yb * cols + k * 512, 512), 512)
            idx = idxo[yb, 0:1, at]
            size, sign = jnp.abs(idx), jnp.where(idx > 0, 1.0, -1.0)

            def some(r, inner):
                base = lax.broadcasted_iota(jnp.int32, (32, 512), 0) + (r * 32 + 1)
                hit = jnp.where(base.astype(f32) == size, sign, 0.0)
                mem_t[pl.ds(pl.multiple_of(r * 32, 32), 32), to] = hit.astype(bf16)
                return inner

            return lax.fori_loop(0, sets // 32, some, carry, unroll=2)

        lax.fori_loop(0, cols // 512, chunk, 0)

    def forward(yb, start, stop):
        def chunk(k, carry):
            at = pl.ds(pl.multiple_of(yb * cols + k * 512, 512), 512)
            sig[:, at] = jnp.dot(half_ref[...], full_ref[:, at], preferred_element_type=f32)

            def some(i, inner):
                part = pl.ds(pl.multiple_of(i * 32, 32), 32)
                v = sig[part, at]
                e = jnp.exp(-jnp.abs(v))
                log = jnp.where(e < 0.01, e * (1.0 - e * (0.5 - e * (1.0 / 3.0))), jnp.log(1.0 + e))
                exposure[part, :] = (jnp.maximum(v, 0.0) + log).astype(bf16)
                d = 1.0 + e
                r = pl.reciprocal(d, approx=True)
                r = r * (2.0 - d * r)
                sig[part, at] = jnp.where(v >= 0, r, e * r)
                return inner

            lax.fori_loop(0, paths // 32, some, 0, unroll=4)
            netted[...] += lax.dot_general(exposure[...], mem_t[:, at], NT, preferred_element_type=f32)
            return carry

        lax.fori_loop(start, stop, chunk, 0)

    def turn():
        for k in range(4):
            size = half_ref.shape[1] // 4
            part = half_ref[:, k * size : (k + 1) * size].astype(f32).T.astype(bf16)
            for n in range(size // rows):
                p = k * (size // rows) + n
                to = ((p // 2) % 2 * 4 + p // 4) * rows
                bt_ref[p % 2, to : to + rows, :] = part[n * rows : (n + 1) * rows, :]

    def spread_far(j):
        own[j][0].wait_recv()
        pass_on(block(line[j], 1 - x, y, 0), gya, 4 + j, to_y)
        pass_on(block(line[j], 1 - x, y, 0), gc, 4 + j, to_c)
        own[j][1].wait_recv()
        pass_on(block(line[j], x, 1 - y, 1), gxb, 4 + j, to_x)
        pass_on(block(line[j], x, 1 - y, 1), gc, 8 + j, to_c)

    netted[...] = jnp.zeros_like(netted)
    zc[0].wait_recv()
    own.append(spread_own(1))
    fetch.wait()
    lax.fori_loop(0, cols // 512, find, 0)
    idx_copy = pass_on(idxo.at[y], gi, 0, to_y)
    spread_far(0)
    build(y)
    zc[1].wait_recv()
    own.append(spread_own(2))
    spread_far(1)
    fetch_half.wait()
    turn()
    idx_copy.wait_recv()
    build(1 - y)
    zc[2].wait_recv()
    own.append(spread_own(3))
    spread_far(2)
    spread_far(3)

    def landed(part, sems, i):
        remote(part, part, sems, i, to_c).wait_recv()
        return part

    def from_core(numbers):
        for i in numbers:
            landed(block(z, x, y) if i < 4 else block(z, x, y, 0), gc, i)

    for j in range(4):
        pass_on(landed(block(line[j], 1 - x, y, 1), gxb, j), gc, 16 + j, to_c)
    for j in range(4):
        pass_on(landed(block(line[j], x, 1 - y, 0), gya, j), gc, 12 + j, to_c)
    from_core([0, 1, 2, 3, 4, 5, 6, 7, 16, 17, 18, 19])
    forward(y, 0, 2)

    def far(j):
        pass_on(landed(block(line[j], 1 - x, 1 - y, 0), gya, 4 + j), gc, 20 + j, to_c)
        pass_on(landed(block(line[j], 1 - x, 1 - y, 1), gxb, 4 + j), gc, 24 + j, to_c)

    far(0)
    far(1)
    far(2)
    far(3)
    forward(y, 2, 4)
    from_core([8, 9, 10, 11, 12, 13, 14, 15, 20, 21, 22, 23, 24, 25, 26, 27])
    forward(1 - y, 0, 4)

    scale, borrow, lend = lax.rsqrt(counts_ref[...].astype(f32)), borrow_ref[...], lend_ref[...]

    def fund(r, carry):
        part = pl.ds(pl.multiple_of(r * 32, 32), 32)
        s = netted[part, :] * scale
        e = jnp.exp(-jnp.abs(s))
        grad = jnp.where(s >= 0, borrow + lend * e, borrow * e + lend) / (1.0 + e) * scale
        set_grad[part, :] = grad.astype(bf16)
        return carry

    lax.fori_loop(0, paths // 32, fund, 0, unroll=4)

    steps = 4
    width = half // steps
    side = rows * 4
    mine, theirs = pl.ds(pl.multiple_of(x * side, side), side), pl.ds(pl.multiple_of((1 - x) * side, side), side)
    copies = {}

    def columns(s, i):
        q = i // 2
        h = lax.rem((i + 1) // 2, 2)
        yq = (1 - y) + q * (2 * y - 1)
        return pl.ds(pl.multiple_of(yq * cols + h * half + s * width, width), width)

    def core_copy(n):
        return remote(cso.at[n], cri.at[n], cs, n, to_c)

    def first_step(s):
        def chunk(i, carry):
            at = columns(s, i)
            grad = jnp.dot(set_grad[...], mem_t[:, at], preferred_element_type=f32)
            vg[:, at] = (grad * sig[:, at]).astype(bf16)
            n = s * 4 + i
            cso[n] = jnp.dot(bt_ref[1 - c], vg[:, at], preferred_element_type=f32).astype(bf16)
            core_copy(n).start()
            return carry

        lax.fori_loop(0, 4, chunk, 0, unroll=2)

    def second_step(s):
        def chunk(i, carry):
            n = s * 4 + i
            own = jnp.dot(bt_ref[c], vg[:, columns(s, i)], preferred_element_type=f32)
            core_copy(n).wait_recv()
            acc[n] = own + cri[n].astype(f32)
            return carry

        lax.fori_loop(0, 4, chunk, 0)
        yso[s] = acc[s * 4].astype(bf16)
        copies["ya", s] = send(yso.at[s], yri.at[s], yas, s, to_y)
        for q in (0, 1):
            j = q * steps + s
            xbo[j] = acc[s * 4 + 1 + q, theirs].astype(bf16)
            copies["xb", j] = send(xbo.at[j], xbi.at[j], xbs, j, to_x)

    def third_step(s):
        copies["xb", s].wait_recv()
        ybo[s] = (acc[s * 4 + 1, mine] + xbi[s].astype(f32)).astype(bf16)
        copies["yb", s] = send(ybo.at[s], ybi.at[s], ybs, s, to_y)
        copies["ya", s].wait_recv()
        xso[s] = (acc[s * 4 + 3, theirs] + yri[s, theirs].astype(f32)).astype(bf16)
        copies["xa", s] = send(xso.at[s], xri.at[s], xas, s, to_x)
        acc[s * 4 + 3, mine] = acc[s * 4 + 3, mine] + yri[s, mine].astype(f32)
        copies["xb", steps + s].wait_recv()
        acc[s * 4 + 2, mine] = acc[s * 4 + 2, mine] + xbi[steps + s].astype(f32)

    def fourth_step(s):
        for h in (1, 0):
            i, j = s * 4 + (2 if h else 3), h * steps + s
            copies["yb" if h else "xa", s].wait_recv()
            arrived = ybi[s] if h else xri[s]
            acc[i, mine] = acc[i, mine] + arrived.astype(f32)
            zso[j] = acc[i, mine].astype(bf16)
            for k in range(3):
                zk = line[k + 1]
                part = zso.at[j, pl.ds(pl.multiple_of(zk * rows, rows), rows)]
                n = k * 2 * steps + j
                copies["z", n] = send(part, zri.at[n], zs, n, device(zk, x, c, y))

    def last_step(s):
        for h in (1, 0):
            i, j = s * 4 + (2 if h else 3), h * steps + s
            total = acc[i, pl.ds(pl.multiple_of(x * side + z * rows, rows), rows)]
            for k in range(3):
                copies["z", k * 2 * steps + j].wait_recv()
                total = total + zri[k * 2 * steps + j].astype(f32)
            out_ref[:, pl.ds(j * width, width)] = total

    def basis_part(n, k):
        size = full_ref.shape[0] // 2
        to, over = slice(k * size, (k + 1) * size), slice(n * cols, (n + 1) * cols)
        db_ref[n, :, to] = lax.dot_general(
            vg[:, over], full_ref[to, over], NT, preferred_element_type=f32
        )

    first_step(0)
    first_step(1)
    second_step(0)
    first_step(2)
    second_step(1)
    third_step(0)
    first_step(3)
    second_step(2)
    fourth_step(0)
    third_step(1)
    second_step(3)
    basis_part(0, 0)
    third_step(2)
    fourth_step(1)
    basis_part(0, 1)
    third_step(3)
    fourth_step(2)
    basis_part(1, 0)
    fourth_step(3)
    basis_part(1, 1)
    for s in range(steps):
        last_step(s)

    def sent(n, carry):
        core_copy(n).wait_send()
        return carry

    lax.fori_loop(0, 4 * steps, sent, 0)
    for copy in started:
        copy.wait_send()


def adjoint(membership, basis, coef, counts, borrow, lend):
    trades, sets = membership.shape
    rows, cols = coef.shape
    paths, k = basis.shape[0] // 2, basis.shape[1]
    b, f = jnp.bfloat16, jnp.float32
    steps = 4
    width, side = cols // 2 // steps, rows * 4
    buffers = [
        ((trades, sets), membership.dtype), ((paths, k), b), ((2, 8 * rows, paths), b), ((k, 2 * cols), b), ((2, 8, cols), f), ((sets, 2 * cols), b),
        ((paths, 2 * cols), f), ((paths, 512), b), ((paths, sets), f), ((paths, sets), b), ((paths, 2 * cols), b),
        ((4 * steps, 2 * side, width), b), ((4 * steps, 2 * side, width), b), ((4 * steps, 2 * side, width), f),
        ((steps, 2 * side, width), b), ((steps, 2 * side, width), b),
        ((steps, side, width), b), ((steps, side, width), b),
        ((2 * steps, side, width), b), ((2 * steps, side, width), b),
        ((steps, side, width), b), ((steps, side, width), b),
        ((2 * steps, side, width), b), ((6 * steps, rows, width), b),
    ]
    lengths = (3, 4, 8, 8, 4, 28, 1, 4 * steps, steps, steps, 2 * steps, steps, 6 * steps)
    sems = [pltpu.SemaphoreType.DMA((n,)) for n in lengths for _ in range(2)]
    return pl.pallas_call(
        adjoint_kernel,
        out_shape=(jax.ShapeDtypeStruct((2, paths, k), f), jax.ShapeDtypeStruct((rows, cols), f)),
        in_specs=[pl.BlockSpec(memory_space=pl.ANY)] * 2 + [VMEM] * 4,
        out_specs=(VMEM, VMEM),
        scratch_shapes=[pltpu.VMEM(shape, kind) for shape, kind in buffers] + [pltpu.SemaphoreType.DMA] * 2 + sems,
        compiler_params=pltpu.CompilerParams(
            collective_id=0, has_side_effects=True, vmem_limit_bytes=50 * 1024 * 1024
        ),
        name="adjoint",
    )(membership, basis, coef, counts, borrow, lend)


def funding(netted, scale, borrow, lend):
    scaled = netted * scale
    grad = (borrow * jax.nn.sigmoid(scaled) + lend * jax.nn.sigmoid(-scaled)) * scale
    return grad.astype(jnp.bfloat16)


def body(basis, coef, membership, counts, borrow, lend):
    row = (1, counts.shape[0])
    parts, total = adjoint(
        membership, basis, coef, counts.reshape(row), borrow.reshape(row), lend.reshape(row)
    )
    factor = (basis.shape[0] * lax.axis_size("paths")) ** -0.5
    return (parts[0] + parts[1], total * factor)


def body_any(basis, coef, membership, counts, borrow, lend):
    path_rows = basis.shape[0]
    member = membership.astype(jnp.bfloat16)
    coef_full = lax.all_gather(coef, "paths", axis=0, tiled=True)
    trade_value = jnp.dot(basis, coef_full, preferred_element_type=jnp.float32)
    exposure = jax.nn.softplus(trade_value).astype(jnp.bfloat16)
    partial_net = jnp.dot(exposure, member, preferred_element_type=jnp.float32)
    scale_all = lax.rsqrt(counts.astype(jnp.float32))
    net_share = lax.psum_scatter(partial_net, "trades", scatter_dimension=1, tiled=True)
    width_sets = net_share.shape[1]
    offset_sets = lax.axis_index("trades") * width_sets
    grad_share = funding(
        net_share,
        lax.dynamic_slice_in_dim(scale_all, offset_sets, width_sets, 0),
        lax.dynamic_slice_in_dim(borrow, offset_sets, width_sets, 0),
        lax.dynamic_slice_in_dim(lend, offset_sets, width_sets, 0),
    )
    set_grad = lax.all_gather(grad_share, "trades", axis=1, tiled=True)
    trade_grad = lax.dot_general(
        set_grad, member, (((1,), (1,)), ((), ())), preferred_element_type=jnp.float32
    )
    value_grad = (trade_grad * jax.nn.sigmoid(trade_value)).astype(jnp.bfloat16)
    d_basis = lax.psum_scatter(
        lax.dot_general(
            value_grad, coef_full, (((1,), (1,)), ((), ())), preferred_element_type=jnp.float32
        ),
        "trades",
        scatter_dimension=0,
        tiled=True,
    )
    factor = 1.0 / jnp.sqrt(jnp.float32(path_rows * lax.axis_size("paths")))
    product = lax.dot_general(
        basis, value_grad, (((0,), (0,)), ((), ())), preferred_element_type=jnp.float32
    )
    d_coef = lax.psum_scatter(product * factor, "paths", scatter_dimension=0, tiled=True)
    return (d_basis, d_coef)


def solution(mesh):
    placed = (P("paths", None), P("paths", "trades"), P("trades", None), P(), P(), P())
    small = (mesh.shape["paths"], mesh.shape["trades"]) == (16, 2)
    return jax.shard_map(
        body if small else body_any,
        mesh=mesh,
        in_specs=placed,
        out_specs=(P(("paths", "trades"), None), P("paths", "trades")),
        check_vma=False,
    )
```

```python
import jax
import jax.numpy as jnp
from jax import lax
from jax.experimental import pallas as pl
from jax.experimental.pallas import tpu as pltpu
from jax.sharding import PartitionSpec as P

MESH = pl.DeviceIdType.MESH
VMEM = pl.BlockSpec(memory_space=pltpu.VMEM)


def place():
    p, y = lax.axis_index("paths"), lax.axis_index("trades")
    return p // 4, lax.rem(p // 2, 2), lax.rem(p, 2), y


def device(z, x, c, y):
    return (z * 4 + x * 2 + c, y)


def greet(z, x, c, y):
    barrier = pltpu.get_barrier_semaphore()
    others = [device(lax.rem(z + k, 4), x, c, y) for k in (1, 2, 3)]
    others += [device(z, 1 - x, c, y), device(z, x, 1 - c, y), device(z, x, c, 1 - y)]
    for other in others:
        pl.semaphore_signal(barrier, inc=1, device_id=other, device_id_type=MESH)
    pl.semaphore_wait(barrier, len(others))


def remote(src, dst, sems, i, target):
    return pltpu.make_async_remote_copy(
        src_ref=src,
        dst_ref=dst,
        send_sem=sems[0].at[i],
        recv_sem=sems[1].at[i],
        device_id=target,
        device_id_type=MESH,
    )


NT = (((1,), (1,)), ((), ()))


def adjoint_kernel(
    member_ref, basis_ref, coef_ref, counts_hbm, borrow_hbm, lend_hbm, db_ref, out_ref,
    counts_ref, borrow_ref, lend_ref,
    member, half_ref, bt_ref, full_ref, idxo, mem_t, sig, exposure, netted, set_grad, vg,
    cso, cri, acc, yso, yri, xso, xri, xbo, xbi, ybo, ybi, zso, zri, fetch_sem, *sems
):
    gz, gxa, gya, gxb, gyb, gc, gi, cs, yas, xas, xbs, ybs, zs = [sems[2 * i : 2 * i + 2] for i in range(13)]
    z, x, c, y = place()
    rows, cols = coef_ref.shape
    half = cols // 2
    paths, sets = netted.shape
    f32, bf16 = jnp.float32, jnp.bfloat16
    started = []

    fetch = pltpu.make_async_copy(member_ref, member, fetch_sem.at[0])
    fetch.start()
    fetch_half = pltpu.make_async_copy(
        basis_ref.at[pl.ds(pl.multiple_of(y * paths, paths), paths)], half_ref, fetch_sem.at[1]
    )
    fetch_half.start()
    small = [
        pltpu.make_async_copy(src, dst, fetch_sem.at[3 + i])
        for i, (src, dst) in enumerate(
            ((counts_hbm, counts_ref), (borrow_hbm, borrow_ref), (lend_hbm, lend_ref))
        )
    ]
    for copy in small:
        copy.start()

    def block(g, zb, xb, yb, h=None):
        row = pl.multiple_of((zb * 4 + xb * 2 + c) * rows, rows)
        size = half if h is None else half // 2
        col = pl.multiple_of(yb * cols + g * half + (h or 0) * size, size)
        return full_ref.at[pl.ds(row, rows), pl.ds(col, size)]

    def send(src, dst, sems, i, target):
        copy = remote(src, dst, sems, i, target)
        copy.start()
        started.append(copy)
        return copy

    def pass_on(part, sems, i, target):
        return send(part, part, sems, i, target)

    to_x, to_y, to_c = device(z, 1 - x, c, y), device(z, x, c, 1 - y), device(z, x, 1 - c, y)
    own_row = pl.multiple_of((z * 4 + x * 2 + c) * rows, rows)
    own_slot = full_ref.at[pl.ds(own_row, rows), pl.ds(pl.multiple_of(y * cols, cols), cols)]
    fetch_coef = pltpu.make_async_copy(coef_ref, own_slot, fetch_sem.at[2])
    fetch_coef.start()
    greet(z, x, c, y)
    fetch_coef.wait()

    near = z + 1 - 2 * lax.rem(z, 2)
    line = [z, near, lax.rem(z + 2, 4), lax.rem(near + 2, 4)]
    zc = [
        [pass_on(block(g, z, x, y), gz, g * 3 + k, device(line[k + 1], x, c, y)) for k in range(3)]
        for g in (0, 1)
    ]
    own = {}

    def spread_own(g, j):
        a = pass_on(block(g, line[j], x, y, 0), gxa, g * 4 + j, to_x)
        b = pass_on(block(g, line[j], x, y, 1), gyb, g * 4 + j, to_y)
        pass_on(block(g, line[j], x, y, 0), gya, g * 8 + j, to_y)
        pass_on(block(g, line[j], x, y, 1), gxb, g * 8 + j, to_x)
        pass_on(block(g, line[j], x, y), gc, g * 28 + j, to_c)
        own[g, j] = a, b

    spread_own(0, 0)

    number = lax.broadcasted_iota(jnp.int32, (16, sets), 1) + 1
    first = lax.broadcasted_iota(jnp.int32, (16, sets), 0) == 0
    digits = jnp.where(first, number // 64, lax.rem(number, 64)).astype(f32).astype(bf16)

    def find(k, carry):
        at = pl.ds(pl.multiple_of(k * 512, 512), 512)
        both = lax.dot_general(
            digits, member[at, :].astype(f32).astype(bf16), NT, preferred_element_type=f32
        )
        idxo[y, :, at] = jnp.broadcast_to(both[0:1] * 64.0 + both[1:2], (8, 512))
        return carry


    def build(yb):
        def chunk(k, carry):
            at = pl.ds(pl.multiple_of(k * 512, 512), 512)
            to = pl.ds(pl.multiple_of(yb * cols + k * 512, 512), 512)
            idx = idxo[yb, 0:1, at]
            size, sign = jnp.abs(idx), jnp.where(idx > 0, 1.0, -1.0)

            def some(r, inner):
                base = lax.broadcasted_iota(jnp.int32, (32, 512), 0) + (r * 32 + 1)
                hit = jnp.where(base.astype(f32) == size, sign, 0.0)
                mem_t[pl.ds(pl.multiple_of(r * 32, 32), 32), to] = hit.astype(bf16)
                return inner

            return lax.fori_loop(0, sets // 32, some, carry, unroll=2)

        lax.fori_loop(0, cols // 512, chunk, 0)

    def forward(yb, start, stop):
        def chunk(k, carry):
            at = pl.ds(pl.multiple_of(yb * cols + k * 512, 512), 512)
            sig[:, at] = jnp.dot(half_ref[...], full_ref[:, at], preferred_element_type=f32)

            def some(i, inner):
                part = pl.ds(pl.multiple_of(i * 32, 32), 32)
                v = sig[part, at]
                e = jnp.exp(-jnp.abs(v))
                log = jnp.where(e < 0.01, e * (1.0 - e * (0.5 - e * (1.0 / 3.0))), jnp.log(1.0 + e))
                exposure[part, :] = (jnp.maximum(v, 0.0) + log).astype(bf16)
                d = 1.0 + e
                r = pl.reciprocal(d, approx=True)
                r = r * (2.0 - d * r)
                sig[part, at] = jnp.where(v >= 0, r, e * r)
                return inner

            lax.fori_loop(0, paths // 32, some, 0, unroll=4)
            netted[...] += lax.dot_general(exposure[...], mem_t[:, at], NT, preferred_element_type=f32)
            return carry

        lax.fori_loop(start, stop, chunk, 0)

    def turn():
        for k in range(4):
            size = half_ref.shape[1] // 4
            part = half_ref[:, k * size : (k + 1) * size].astype(f32).T.astype(bf16)
            for n in range(size // rows):
                p = k * (size // rows) + n
                to = ((p // 2) % 2 * 4 + p // 4) * rows
                bt_ref[p % 2, to : to + rows, :] = part[n * rows : (n + 1) * rows, :]

    def spread_far(g, j):
        own[g, j][0].wait_recv()
        pass_on(block(g, line[j], 1 - x, y, 0), gya, g * 8 + 4 + j, to_y)
        pass_on(block(g, line[j], 1 - x, y, 0), gc, g * 28 + 4 + j, to_c)
        own[g, j][1].wait_recv()
        pass_on(block(g, line[j], x, 1 - y, 1), gxb, g * 8 + 4 + j, to_x)
        pass_on(block(g, line[j], x, 1 - y, 1), gc, g * 28 + 8 + j, to_c)

    def landed(part, sems, i):
        remote(part, part, sems, i, to_c).wait_recv()
        return part

    def from_core(g, numbers):
        for i in numbers:
            landed(block(g, z, x, y) if i < 4 else block(g, z, x, y, 0), gc, g * 28 + i)

    def to_core(g):
        for j in range(4):
            pass_on(landed(block(g, line[j], 1 - x, y, 1), gxb, g * 8 + j), gc, g * 28 + 16 + j, to_c)
            pass_on(landed(block(g, line[j], x, 1 - y, 0), gya, g * 8 + j), gc, g * 28 + 12 + j, to_c)

    def far(g, j):
        pass_on(landed(block(g, line[j], 1 - x, 1 - y, 0), gya, g * 8 + 4 + j), gc, g * 28 + 20 + j, to_c)
        pass_on(landed(block(g, line[j], 1 - x, 1 - y, 1), gxb, g * 8 + 4 + j), gc, g * 28 + 24 + j, to_c)

    near_core = [0, 1, 2, 3, 4, 5, 6, 7, 16, 17, 18, 19]
    far_core = [8, 9, 10, 11, 12, 13, 14, 15, 20, 21, 22, 23, 24, 25, 26, 27]

    netted[...] = jnp.zeros_like(netted)
    zc[0][0].wait_recv()
    spread_own(0, 1)
    fetch.wait()
    lax.fori_loop(0, cols // 512, find, 0)
    idx_copy = pass_on(idxo.at[y], gi, 0, to_y)
    spread_far(0, 0)
    zc[0][1].wait_recv()
    spread_own(0, 2)
    spread_far(0, 1)
    spread_own(1, 0)
    fetch_half.wait()
    turn()
    zc[0][2].wait_recv()
    spread_own(0, 3)
    spread_far(0, 2)
    build(y)
    spread_far(0, 3)
    to_core(0)
    zc[1][0].wait_recv()
    spread_own(1, 1)
    spread_far(1, 0)
    for j in range(4):
        far(0, j)
    zc[1][1].wait_recv()
    spread_own(1, 2)
    spread_far(1, 1)
    from_core(0, near_core)
    forward(y, 0, 1)
    zc[1][2].wait_recv()
    spread_own(1, 3)
    spread_far(1, 2)
    idx_copy.wait_recv()
    build(1 - y)
    spread_far(1, 3)
    forward(y, 1, 2)
    to_core(1)
    from_core(0, far_core)
    forward(1 - y, 0, 1)
    far(1, 0)
    far(1, 1)
    forward(1 - y, 1, 2)
    far(1, 2)
    far(1, 3)
    from_core(1, near_core)
    forward(y, 2, 4)
    from_core(1, far_core)
    forward(1 - y, 2, 4)

    for copy in small:
        copy.wait()
    scale, borrow, lend = lax.rsqrt(counts_ref[...].astype(f32)), borrow_ref[...], lend_ref[...]

    def fund(r, carry):
        part = pl.ds(pl.multiple_of(r * 32, 32), 32)
        s = netted[part, :] * scale
        e = jnp.exp(-jnp.abs(s))
        grad = jnp.where(s >= 0, borrow + lend * e, borrow * e + lend) / (1.0 + e) * scale
        set_grad[part, :] = grad.astype(bf16)
        return carry

    lax.fori_loop(0, paths // 32, fund, 0, unroll=4)

    steps = 4
    width = half // steps
    side = rows * 4
    mine, theirs = pl.ds(pl.multiple_of(x * side, side), side), pl.ds(pl.multiple_of((1 - x) * side, side), side)
    copies = {}

    def columns(s, i):
        q = i // 2
        h = lax.rem((i + 1) // 2, 2)
        yq = (1 - y) + q * (2 * y - 1)
        return pl.ds(pl.multiple_of(yq * cols + h * half + s * width, width), width)

    def core_copy(n):
        return remote(cso.at[n], cri.at[n], cs, n, to_c)

    def first_step(s):
        def chunk(i, carry):
            at = columns(s, i)
            grad = jnp.dot(set_grad[...], mem_t[:, at], preferred_element_type=f32)
            vg[:, at] = (grad * sig[:, at]).astype(bf16)
            n = s * 4 + i
            cso[n] = jnp.dot(bt_ref[1 - c], vg[:, at], preferred_element_type=f32).astype(bf16)
            core_copy(n).start()
            return carry

        lax.fori_loop(0, 4, chunk, 0, unroll=2)

    def second_step(s):
        def chunk(i, carry):
            n = s * 4 + i
            own = jnp.dot(bt_ref[c], vg[:, columns(s, i)], preferred_element_type=f32)
            core_copy(n).wait_recv()
            acc[n] = own + cri[n].astype(f32)
            return carry

        lax.fori_loop(0, 4, chunk, 0)
        yso[s] = acc[s * 4].astype(bf16)
        copies["ya", s] = send(yso.at[s], yri.at[s], yas, s, to_y)
        for q in (0, 1):
            j = q * steps + s
            xbo[j] = acc[s * 4 + 1 + q, theirs].astype(bf16)
            copies["xb", j] = send(xbo.at[j], xbi.at[j], xbs, j, to_x)

    def third_step(s):
        copies["xb", s].wait_recv()
        ybo[s] = (acc[s * 4 + 1, mine] + xbi[s].astype(f32)).astype(bf16)
        copies["yb", s] = send(ybo.at[s], ybi.at[s], ybs, s, to_y)
        copies["ya", s].wait_recv()
        xso[s] = (acc[s * 4 + 3, theirs] + yri[s, theirs].astype(f32)).astype(bf16)
        copies["xa", s] = send(xso.at[s], xri.at[s], xas, s, to_x)
        acc[s * 4 + 3, mine] = acc[s * 4 + 3, mine] + yri[s, mine].astype(f32)
        copies["xb", steps + s].wait_recv()
        acc[s * 4 + 2, mine] = acc[s * 4 + 2, mine] + xbi[steps + s].astype(f32)

    def fourth_step(s):
        for h in (1, 0):
            i, j = s * 4 + (2 if h else 3), h * steps + s
            copies["yb" if h else "xa", s].wait_recv()
            arrived = ybi[s] if h else xri[s]
            acc[i, mine] = acc[i, mine] + arrived.astype(f32)
            zso[j] = acc[i, mine].astype(bf16)
            for k in range(3):
                zk = line[k + 1]
                part = zso.at[j, pl.ds(pl.multiple_of(zk * rows, rows), rows)]
                n = k * 2 * steps + j
                copies["z", n] = send(part, zri.at[n], zs, n, device(zk, x, c, y))

    def last_step(s):
        for h in (1, 0):
            i, j = s * 4 + (2 if h else 3), h * steps + s
            total = acc[i, pl.ds(pl.multiple_of(x * side + z * rows, rows), rows)]
            for k in range(3):
                copies["z", k * 2 * steps + j].wait_recv()
                total = total + zri[k * 2 * steps + j].astype(f32)
            out_ref[:, pl.ds(j * width, width)] = total

    def basis_part(n, k):
        size = full_ref.shape[0] // 2
        to, over = slice(k * size, (k + 1) * size), slice(n * cols, (n + 1) * cols)
        db_ref[n, :, to] = lax.dot_general(
            vg[:, over], full_ref[to, over], NT, preferred_element_type=f32
        )

    first_step(0)
    first_step(1)
    second_step(0)
    first_step(2)
    second_step(1)
    third_step(0)
    first_step(3)
    second_step(2)
    fourth_step(0)
    third_step(1)
    second_step(3)
    basis_part(0, 0)
    third_step(2)
    fourth_step(1)
    basis_part(0, 1)
    third_step(3)
    fourth_step(2)
    basis_part(1, 0)
    fourth_step(3)
    basis_part(1, 1)
    for s in range(steps):
        last_step(s)

    def sent(n, carry):
        core_copy(n).wait_send()
        return carry

    lax.fori_loop(0, 4 * steps, sent, 0)
    for copy in started:
        copy.wait_send()


def adjoint(membership, basis, coef, counts, borrow, lend):
    trades, sets = membership.shape
    rows, cols = coef.shape
    paths, k = basis.shape[0] // 2, basis.shape[1]
    b, f = jnp.bfloat16, jnp.float32
    steps = 4
    width, side = cols // 2 // steps, rows * 4
    buffers = [
        ((1, sets), counts.dtype), ((1, sets), f), ((1, sets), f), ((trades, sets), membership.dtype), ((paths, k), b), ((2, 8 * rows, paths), b), ((k, 2 * cols), b), ((2, 8, cols), f), ((sets, 2 * cols), b),
        ((paths, 2 * cols), f), ((paths, 512), b), ((paths, sets), f), ((paths, sets), b), ((paths, 2 * cols), b),
        ((4 * steps, 2 * side, width), b), ((4 * steps, 2 * side, width), b), ((4 * steps, 2 * side, width), f),
        ((steps, 2 * side, width), b), ((steps, 2 * side, width), b),
        ((steps, side, width), b), ((steps, side, width), b),
        ((2 * steps, side, width), b), ((2 * steps, side, width), b),
        ((steps, side, width), b), ((steps, side, width), b),
        ((2 * steps, side, width), b), ((6 * steps, rows, width), b),
    ]
    lengths = (6, 8, 16, 16, 8, 56, 1, 4 * steps, steps, steps, 2 * steps, steps, 6 * steps)
    sems = [pltpu.SemaphoreType.DMA((n,)) for n in lengths for _ in range(2)]
    return pl.pallas_call(
        adjoint_kernel,
        out_shape=(jax.ShapeDtypeStruct((2, paths, k), f), jax.ShapeDtypeStruct((rows, cols), f)),
        in_specs=[pl.BlockSpec(memory_space=pltpu.HBM)] * 6,
        out_specs=(VMEM, VMEM),
        scratch_shapes=[pltpu.VMEM(shape, kind) for shape, kind in buffers] + [pltpu.SemaphoreType.DMA((6,))] + sems,
        compiler_params=pltpu.CompilerParams(
            collective_id=0, has_side_effects=True, vmem_limit_bytes=56 * 1024 * 1024
        ),
        name="adjoint",
    )(membership, basis, coef, counts, borrow, lend)


def funding(netted, scale, borrow, lend):
    scaled = netted * scale
    grad = (borrow * jax.nn.sigmoid(scaled) + lend * jax.nn.sigmoid(-scaled)) * scale
    return grad.astype(jnp.bfloat16)


def body(basis, coef, membership, counts, borrow, lend):
    row = (1, counts.shape[0])
    parts, total = adjoint(
        membership, basis, coef, counts.reshape(row), borrow.reshape(row), lend.reshape(row)
    )
    factor = (basis.shape[0] * lax.axis_size("paths")) ** -0.5
    return (parts[0] + parts[1], total * factor)


def body_any(basis, coef, membership, counts, borrow, lend):
    path_rows = basis.shape[0]
    member = membership.astype(jnp.bfloat16)
    coef_full = lax.all_gather(coef, "paths", axis=0, tiled=True)
    trade_value = jnp.dot(basis, coef_full, preferred_element_type=jnp.float32)
    exposure = jax.nn.softplus(trade_value).astype(jnp.bfloat16)
    partial_net = jnp.dot(exposure, member, preferred_element_type=jnp.float32)
    scale_all = lax.rsqrt(counts.astype(jnp.float32))
    net_share = lax.psum_scatter(partial_net, "trades", scatter_dimension=1, tiled=True)
    width_sets = net_share.shape[1]
    offset_sets = lax.axis_index("trades") * width_sets
    grad_share = funding(
        net_share,
        lax.dynamic_slice_in_dim(scale_all, offset_sets, width_sets, 0),
        lax.dynamic_slice_in_dim(borrow, offset_sets, width_sets, 0),
        lax.dynamic_slice_in_dim(lend, offset_sets, width_sets, 0),
    )
    set_grad = lax.all_gather(grad_share, "trades", axis=1, tiled=True)
    trade_grad = lax.dot_general(
        set_grad, member, (((1,), (1,)), ((), ())), preferred_element_type=jnp.float32
    )
    value_grad = (trade_grad * jax.nn.sigmoid(trade_value)).astype(jnp.bfloat16)
    d_basis = lax.psum_scatter(
        lax.dot_general(
            value_grad, coef_full, (((1,), (1,)), ((), ())), preferred_element_type=jnp.float32
        ),
        "trades",
        scatter_dimension=0,
        tiled=True,
    )
    factor = 1.0 / jnp.sqrt(jnp.float32(path_rows * lax.axis_size("paths")))
    product = lax.dot_general(
        basis, value_grad, (((0,), (0,)), ((), ())), preferred_element_type=jnp.float32
    )
    d_coef = lax.psum_scatter(product * factor, "paths", scatter_dimension=0, tiled=True)
    return (d_basis, d_coef)


def solution(mesh):
    placed = (P("paths", None), P("paths", "trades"), P("trades", None), P(), P(), P())
    small = (mesh.shape["paths"], mesh.shape["trades"]) == (16, 2)
    return jax.shard_map(
        body if small else body_any,
        mesh=mesh,
        in_specs=placed,
        out_specs=(P(("paths", "trades"), None), P("paths", "trades")),
        check_vma=False,
    )
```

```python
import functools

import jax
import jax.numpy as jnp
from jax import lax
from jax.experimental import pallas as pl
from jax.experimental.pallas import tpu as pltpu
from jax.sharding import PartitionSpec as P

MESH = pl.DeviceIdType.MESH
VMEM = pl.BlockSpec(memory_space=pltpu.VMEM)


def place():
    p, y = lax.axis_index("paths"), lax.axis_index("trades")
    return p // 4, lax.rem(p // 2, 2), lax.rem(p, 2), y


def device(z, x, c, y):
    return (z * 4 + x * 2 + c, y)


def greet(z, x, c, y):
    barrier = pltpu.get_barrier_semaphore()
    others = [device(lax.rem(z + k, 4), x, c, y) for k in (1, 2, 3)]
    others += [device(z, 1 - x, c, y), device(z, x, 1 - c, y), device(z, x, c, 1 - y)]
    for other in others:
        pl.semaphore_signal(barrier, inc=1, device_id=other, device_id_type=MESH)
    pl.semaphore_wait(barrier, len(others))


def remote(src, dst, sems, i, target):
    return pltpu.make_async_remote_copy(
        src_ref=src,
        dst_ref=dst,
        send_sem=sems[0].at[i],
        recv_sem=sems[1].at[i],
        device_id=target,
        device_id_type=MESH,
    )


NT = (((1,), (1,)), ((), ()))


def adjoint_kernel(
    member_ref, basis_ref, coef_ref, counts_hbm, borrow_hbm, lend_hbm, db_ref, out_ref,
    counts_ref, borrow_ref, lend_ref,
    member, half_ref, bt_ref, full_ref, idxo, mem_t, sig, exposure, netted, set_grad, vg,
    cso, cri, acc, yso, yri, xso, xri, xbo, xbi, ybo, ybi, zso, zri, fetch_sem, *sems
):
    gz, gxa, gya, gxb, gyb, gc, gi, cs, yas, xas, xbs, ybs, zs = [sems[2 * i : 2 * i + 2] for i in range(13)]
    z, x, c, y = place()
    rows, cols = coef_ref.shape
    half = cols // 2
    paths, sets = netted.shape
    f32, bf16 = jnp.float32, jnp.bfloat16
    started = []

    fetch = pltpu.make_async_copy(member_ref, member, fetch_sem.at[0])
    fetch.start()
    fetch_half = pltpu.make_async_copy(
        basis_ref.at[pl.ds(pl.multiple_of(y * paths, paths), paths)], half_ref, fetch_sem.at[1]
    )
    fetch_half.start()
    small = [
        pltpu.make_async_copy(src, dst, fetch_sem.at[3 + i])
        for i, (src, dst) in enumerate(
            ((counts_hbm, counts_ref), (borrow_hbm, borrow_ref), (lend_hbm, lend_ref))
        )
    ]
    for copy in small:
        copy.start()

    def block(g, zb, xb, yb, h=None):
        row = pl.multiple_of((zb * 4 + xb * 2 + c) * rows, rows)
        size = half if h is None else half // 2
        col = pl.multiple_of(yb * cols + g * half + (h or 0) * size, size)
        return full_ref.at[pl.ds(row, rows), pl.ds(col, size)]

    def send(src, dst, sems, i, target):
        copy = remote(src, dst, sems, i, target)
        copy.start()
        started.append(copy)
        return copy

    def pass_on(part, sems, i, target):
        return send(part, part, sems, i, target)

    to_x, to_y, to_c = device(z, 1 - x, c, y), device(z, x, c, 1 - y), device(z, x, 1 - c, y)
    own_row = pl.multiple_of((z * 4 + x * 2 + c) * rows, rows)
    own_slot = full_ref.at[pl.ds(own_row, rows), pl.ds(pl.multiple_of(y * cols, cols), cols)]
    fetch_coef = pltpu.make_async_copy(coef_ref, own_slot, fetch_sem.at[2])
    fetch_coef.start()
    greet(z, x, c, y)
    fetch_coef.wait()

    near = z + 1 - 2 * lax.rem(z, 2)
    line = [z, near, lax.rem(z + 2, 4), lax.rem(near + 2, 4)]
    zc = [
        [pass_on(block(g, z, x, y), gz, g * 3 + k, device(line[k + 1], x, c, y)) for k in range(3)]
        for g in (0, 1)
    ]
    own = {}

    def spread_own(g, j):
        a = pass_on(block(g, line[j], x, y, 0), gxa, g * 4 + j, to_x)
        b = pass_on(block(g, line[j], x, y, 1), gyb, g * 4 + j, to_y)
        pass_on(block(g, line[j], x, y, 0), gya, g * 8 + j, to_y)
        pass_on(block(g, line[j], x, y, 1), gxb, g * 8 + j, to_x)
        pass_on(block(g, line[j], x, y), gc, g * 28 + j, to_c)
        own[g, j] = a, b

    spread_own(0, 0)

    number = lax.broadcasted_iota(jnp.int32, (16, sets), 1) + 1
    first = lax.broadcasted_iota(jnp.int32, (16, sets), 0) == 0
    digits = jnp.where(first, number // 64, lax.rem(number, 64)).astype(f32).astype(bf16)

    def find(k, carry):
        at = pl.ds(pl.multiple_of(k * 512, 512), 512)
        both = lax.dot_general(
            digits, member[at, :].astype(f32).astype(bf16), NT, preferred_element_type=f32
        )
        idxo[y, :, at] = jnp.broadcast_to(both[0:1] * 64.0 + both[1:2], (8, 512))
        return carry


    def build(yb):
        def chunk(k, carry):
            at = pl.ds(pl.multiple_of(k * 512, 512), 512)
            to = pl.ds(pl.multiple_of(yb * cols + k * 512, 512), 512)
            idx = idxo[yb, 0:1, at]
            size, sign = jnp.abs(idx), jnp.where(idx > 0, 1.0, -1.0)

            def some(r, inner):
                base = lax.broadcasted_iota(jnp.int32, (32, 512), 0) + (r * 32 + 1)
                hit = jnp.where(base.astype(f32) == size, sign, 0.0)
                mem_t[pl.ds(pl.multiple_of(r * 32, 32), 32), to] = hit.astype(bf16)
                return inner

            return lax.fori_loop(0, sets // 32, some, carry, unroll=2)

        lax.fori_loop(0, cols // 512, chunk, 0)

    def forward(yb, start, stop):
        def chunk(k, carry):
            at = pl.ds(pl.multiple_of(yb * cols + k * 512, 512), 512)
            sig[:, at] = jnp.dot(half_ref[...], full_ref[:, at], preferred_element_type=f32)

            def some(i, inner):
                part = pl.ds(pl.multiple_of(i * 32, 32), 32)
                v = sig[part, at]
                e = jnp.exp(-jnp.abs(v))
                log = jnp.where(e < 0.01, e * (1.0 - e * (0.5 - e * (1.0 / 3.0))), jnp.log(1.0 + e))
                exposure[part, :] = (jnp.maximum(v, 0.0) + log).astype(bf16)
                d = 1.0 + e
                r = pl.reciprocal(d, approx=True)
                r = r * (2.0 - d * r)
                sig[part, at] = jnp.where(v >= 0, r, e * r)
                return inner

            lax.fori_loop(0, paths // 32, some, 0, unroll=4)
            netted[...] += lax.dot_general(exposure[...], mem_t[:, at], NT, preferred_element_type=f32)
            return carry

        lax.fori_loop(start, stop, chunk, 0)

    def turn():
        for k in range(4):
            size = half_ref.shape[1] // 4
            part = half_ref[:, k * size : (k + 1) * size].astype(f32).T.astype(bf16)
            for n in range(size // rows):
                p = k * (size // rows) + n
                to = ((p // 2) % 2 * 4 + p // 4) * rows
                bt_ref[p % 2, to : to + rows, :] = part[n * rows : (n + 1) * rows, :]

    def spread_far(g, j):
        own[g, j][0].wait_recv()
        pass_on(block(g, line[j], 1 - x, y, 0), gya, g * 8 + 4 + j, to_y)
        pass_on(block(g, line[j], 1 - x, y, 0), gc, g * 28 + 4 + j, to_c)
        own[g, j][1].wait_recv()
        pass_on(block(g, line[j], x, 1 - y, 1), gxb, g * 8 + 4 + j, to_x)
        pass_on(block(g, line[j], x, 1 - y, 1), gc, g * 28 + 8 + j, to_c)

    def landed(part, sems, i):
        remote(part, part, sems, i, to_c).wait_recv()
        return part

    def from_core(g, numbers):
        for i in numbers:
            landed(block(g, z, x, y) if i < 4 else block(g, z, x, y, 0), gc, g * 28 + i)

    def to_core(g):
        for j in range(4):
            pass_on(landed(block(g, line[j], 1 - x, y, 1), gxb, g * 8 + j), gc, g * 28 + 16 + j, to_c)
            pass_on(landed(block(g, line[j], x, 1 - y, 0), gya, g * 8 + j), gc, g * 28 + 12 + j, to_c)

    def far(g, j):
        pass_on(landed(block(g, line[j], 1 - x, 1 - y, 0), gya, g * 8 + 4 + j), gc, g * 28 + 20 + j, to_c)
        pass_on(landed(block(g, line[j], 1 - x, 1 - y, 1), gxb, g * 8 + 4 + j), gc, g * 28 + 24 + j, to_c)

    near_core = [0, 1, 2, 3, 4, 5, 6, 7, 16, 17, 18, 19]
    far_core = [8, 9, 10, 11, 12, 13, 14, 15, 20, 21, 22, 23, 24, 25, 26, 27]

    netted[...] = jnp.zeros_like(netted)
    zc[0][0].wait_recv()
    spread_own(0, 1)
    fetch.wait()
    lax.fori_loop(0, cols // 512, find, 0)
    idx_copy = pass_on(idxo.at[y], gi, 0, to_y)
    spread_far(0, 0)
    zc[0][1].wait_recv()
    spread_own(0, 2)
    spread_far(0, 1)
    spread_own(1, 0)
    fetch_half.wait()
    turn()
    zc[0][2].wait_recv()
    spread_own(0, 3)
    spread_far(0, 2)
    build(y)
    spread_far(0, 3)
    to_core(0)
    zc[1][0].wait_recv()
    spread_own(1, 1)
    spread_far(1, 0)
    for j in range(4):
        far(0, j)
    zc[1][1].wait_recv()
    spread_own(1, 2)
    spread_far(1, 1)
    from_core(0, near_core)
    zc[1][2].wait_recv()
    spread_own(1, 3)
    spread_far(1, 2)
    idx_copy.wait_recv()
    build(1 - y)
    spread_far(1, 3)
    forward(y, 0, 2)
    to_core(1)
    from_core(0, far_core)
    far(1, 0)
    far(1, 1)
    forward(1 - y, 0, 2)
    far(1, 2)
    far(1, 3)
    from_core(1, near_core)
    forward(y, 2, 4)
    from_core(1, far_core)
    forward(1 - y, 2, 4)

    for copy in small:
        copy.wait()
    scale, borrow, lend = lax.rsqrt(counts_ref[...].astype(f32)), borrow_ref[...], lend_ref[...]

    def fund(r, carry):
        part = pl.ds(pl.multiple_of(r * 32, 32), 32)
        s = netted[part, :] * scale
        e = jnp.exp(-jnp.abs(s))
        grad = jnp.where(s >= 0, borrow + lend * e, borrow * e + lend) / (1.0 + e) * scale
        set_grad[part, :] = grad.astype(bf16)
        return carry

    lax.fori_loop(0, paths // 32, fund, 0, unroll=4)

    steps = 4
    width = half // steps
    side = rows * 4
    mine, theirs = pl.ds(pl.multiple_of(x * side, side), side), pl.ds(pl.multiple_of((1 - x) * side, side), side)

    def columns(s, i):
        q = i // 2
        h = lax.rem((i + 1) // 2, 2)
        yq = (1 - y) + q * (2 * y - 1)
        return pl.ds(pl.multiple_of(yq * cols + h * half + s * width, width), width)

    def core_copy(n):
        return remote(cso.at[n], cri.at[n], cs, n, to_c)

    def first_step(s):
        def chunk(i, carry):
            at = columns(s, i)
            grad = jnp.dot(set_grad[...], mem_t[:, at], preferred_element_type=f32)
            vg[:, at] = (grad * sig[:, at]).astype(bf16)
            n = s * 4 + i
            cso[n] = jnp.dot(bt_ref[1 - c], vg[:, at], preferred_element_type=f32).astype(bf16)
            core_copy(n).start()
            return carry

        lax.fori_loop(0, 4, chunk, 0, unroll=2)

    def second_step(s):
        def chunk(i, carry):
            n = s * 4 + i
            own = jnp.dot(bt_ref[c], vg[:, columns(s, i)], preferred_element_type=f32)
            core_copy(n).wait_recv()
            acc[n] = own + cri[n].astype(f32)
            return carry

        lax.fori_loop(0, 4, chunk, 0)
        yso[s] = acc[s * 4].astype(bf16)
        ya_copy(s).start()
        for q in (0, 1):
            j = q * steps + s
            xbo[j] = acc[s * 4 + 1 + q, theirs].astype(bf16)
            xb_copy(j).start()

    def ya_copy(s):
        return remote(yso.at[s], yri.at[s], yas, s, to_y)

    def xb_copy(j):
        return remote(xbo.at[j], xbi.at[j], xbs, j, to_x)

    def yb_copy(s):
        return remote(ybo.at[s], ybi.at[s], ybs, s, to_y)

    def xa_copy(s):
        return remote(xso.at[s], xri.at[s], xas, s, to_x)

    def z_copy(k, j):
        zk = line[k + 1]
        part = zso.at[j, pl.ds(pl.multiple_of(zk * rows, rows), rows)]
        n = k * 2 * steps + j
        return remote(part, zri.at[n], zs, n, device(zk, x, c, y))

    def third_step(s):
        xb_copy(s).wait_recv()
        ybo[s] = (acc[s * 4 + 1, mine] + xbi[s].astype(f32)).astype(bf16)
        yb_copy(s).start()
        ya_copy(s).wait_recv()
        xso[s] = (acc[s * 4 + 3, theirs] + yri[s, theirs].astype(f32)).astype(bf16)
        xa_copy(s).start()
        acc[s * 4 + 3, mine] = acc[s * 4 + 3, mine] + yri[s, mine].astype(f32)
        xb_copy(steps + s).wait_recv()
        acc[s * 4 + 2, mine] = acc[s * 4 + 2, mine] + xbi[steps + s].astype(f32)

    def fourth_step(s):
        for h in (1, 0):
            i, j = s * 4 + (2 if h else 3), h * steps + s
            (yb_copy(s) if h else xa_copy(s)).wait_recv()
            arrived = ybi[s] if h else xri[s]
            acc[i, mine] = acc[i, mine] + arrived.astype(f32)
            zso[j] = acc[i, mine].astype(bf16)
            for k in range(3):
                z_copy(k, j).start()

    def last_step(s):
        for h in (1, 0):
            i, j = s * 4 + (2 if h else 3), h * steps + s
            total = acc[i, pl.ds(pl.multiple_of(x * side + z * rows, rows), rows)]
            for k in range(3):
                z_copy(k, j).wait_recv()
                total = total + zri[k * 2 * steps + j].astype(f32)
            out_ref[:, pl.ds(j * width, width)] = total

    def basis_part(i):
        n, k = i // 2, lax.rem(i, 2)
        size = full_ref.shape[0] // 2
        to = pl.ds(pl.multiple_of(k * size, size), size)
        over = pl.ds(pl.multiple_of(n * cols, cols), cols)
        db_ref[n, :, to] = lax.dot_general(
            vg[:, over], full_ref[to, over], NT, preferred_element_type=f32
        )

    def stage(m, carry):
        for lag, step in enumerate((first_step, second_step, third_step, fourth_step)):
            pl.when((m >= lag) & (m < lag + steps))(functools.partial(step, m - lag))
        pl.when(m >= 3)(functools.partial(basis_part, m - 3))
        return carry

    lax.fori_loop(0, steps + 3, stage, 0)
    for s in range(steps):
        last_step(s)

    def sent(n, carry):
        core_copy(n).wait_send()
        return carry

    lax.fori_loop(0, 4 * steps, sent, 0)

    def sent_later(s, carry):
        for copy in (ya_copy(s), xa_copy(s), yb_copy(s), xb_copy(s), xb_copy(steps + s)):
            copy.wait_send()
        for k in range(3):
            z_copy(k, s).wait_send()
            z_copy(k, steps + s).wait_send()
        return carry

    lax.fori_loop(0, steps, sent_later, 0)
    for copy in started:
        copy.wait_send()


def adjoint(membership, basis, coef, counts, borrow, lend):
    trades, sets = membership.shape
    rows, cols = coef.shape
    paths, k = basis.shape[0] // 2, basis.shape[1]
    b, f = jnp.bfloat16, jnp.float32
    steps = 4
    width, side = cols // 2 // steps, rows * 4
    buffers = [
        ((1, sets), counts.dtype), ((1, sets), f), ((1, sets), f), ((trades, sets), membership.dtype), ((paths, k), b), ((2, 8 * rows, paths), b), ((k, 2 * cols), b), ((2, 8, cols), f), ((sets, 2 * cols), b),
        ((paths, 2 * cols), f), ((paths, 512), b), ((paths, sets), f), ((paths, sets), b), ((paths, 2 * cols), b),
        ((4 * steps, 2 * side, width), b), ((4 * steps, 2 * side, width), b), ((4 * steps, 2 * side, width), f),
        ((steps, 2 * side, width), b), ((steps, 2 * side, width), b),
        ((steps, side, width), b), ((steps, side, width), b),
        ((2 * steps, side, width), b), ((2 * steps, side, width), b),
        ((steps, side, width), b), ((steps, side, width), b),
        ((2 * steps, side, width), b), ((6 * steps, rows, width), b),
    ]
    lengths = (6, 8, 16, 16, 8, 56, 1, 4 * steps, steps, steps, 2 * steps, steps, 6 * steps)
    sems = [pltpu.SemaphoreType.DMA((n,)) for n in lengths for _ in range(2)]
    return pl.pallas_call(
        adjoint_kernel,
        out_shape=(jax.ShapeDtypeStruct((2, paths, k), f), jax.ShapeDtypeStruct((rows, cols), f)),
        in_specs=[pl.BlockSpec(memory_space=pltpu.HBM)] * 6,
        out_specs=(VMEM, VMEM),
        scratch_shapes=[pltpu.VMEM(shape, kind) for shape, kind in buffers] + [pltpu.SemaphoreType.DMA((6,))] + sems,
        compiler_params=pltpu.CompilerParams(
            collective_id=0, has_side_effects=True, vmem_limit_bytes=56 * 1024 * 1024
        ),
        name="adjoint",
    )(membership, basis, coef, counts, borrow, lend)


def funding(netted, scale, borrow, lend):
    scaled = netted * scale
    grad = (borrow * jax.nn.sigmoid(scaled) + lend * jax.nn.sigmoid(-scaled)) * scale
    return grad.astype(jnp.bfloat16)


def body(basis, coef, membership, counts, borrow, lend):
    row = (1, counts.shape[0])
    parts, total = adjoint(
        membership, basis, coef, counts.reshape(row), borrow.reshape(row), lend.reshape(row)
    )
    factor = (basis.shape[0] * lax.axis_size("paths")) ** -0.5
    return (parts[0] + parts[1], total * factor)


def body_any(basis, coef, membership, counts, borrow, lend):
    path_rows = basis.shape[0]
    member = membership.astype(jnp.bfloat16)
    coef_full = lax.all_gather(coef, "paths", axis=0, tiled=True)
    trade_value = jnp.dot(basis, coef_full, preferred_element_type=jnp.float32)
    exposure = jax.nn.softplus(trade_value).astype(jnp.bfloat16)
    partial_net = jnp.dot(exposure, member, preferred_element_type=jnp.float32)
    scale_all = lax.rsqrt(counts.astype(jnp.float32))
    net_share = lax.psum_scatter(partial_net, "trades", scatter_dimension=1, tiled=True)
    width_sets = net_share.shape[1]
    offset_sets = lax.axis_index("trades") * width_sets
    grad_share = funding(
        net_share,
        lax.dynamic_slice_in_dim(scale_all, offset_sets, width_sets, 0),
        lax.dynamic_slice_in_dim(borrow, offset_sets, width_sets, 0),
        lax.dynamic_slice_in_dim(lend, offset_sets, width_sets, 0),
    )
    set_grad = lax.all_gather(grad_share, "trades", axis=1, tiled=True)
    trade_grad = lax.dot_general(
        set_grad, member, (((1,), (1,)), ((), ())), preferred_element_type=jnp.float32
    )
    value_grad = (trade_grad * jax.nn.sigmoid(trade_value)).astype(jnp.bfloat16)
    d_basis = lax.psum_scatter(
        lax.dot_general(
            value_grad, coef_full, (((1,), (1,)), ((), ())), preferred_element_type=jnp.float32
        ),
        "trades",
        scatter_dimension=0,
        tiled=True,
    )
    factor = 1.0 / jnp.sqrt(jnp.float32(path_rows * lax.axis_size("paths")))
    product = lax.dot_general(
        basis, value_grad, (((0,), (0,)), ((), ())), preferred_element_type=jnp.float32
    )
    d_coef = lax.psum_scatter(product * factor, "paths", scatter_dimension=0, tiled=True)
    return (d_basis, d_coef)


def solution(mesh):
    placed = (P("paths", None), P("paths", "trades"), P("trades", None), P(), P(), P())
    small = (mesh.shape["paths"], mesh.shape["trades"]) == (16, 2)
    return jax.shard_map(
        body if small else body_any,
        mesh=mesh,
        in_specs=placed,
        out_specs=(P(("paths", "trades"), None), P("paths", "trades")),
        check_vma=False,
    )
```
